32 devices in a mesh: dp: 8 (over y, x, core), mp: 4 (over z).
Axes of the slice: x: 2, y: 2, z: 4, core: 2. Of those that a mesh axis runs over, the one named last changes fastest.
Arguments:
- tokens: bfloat16 [32768, 768], P(('dp', 'mp')), may hold values from -6 to 6
- block_kind: int32 [64], P(('dp', 'mp')), may hold values from 0 to 2
- ln1_gain: bfloat16 [768], replicated, may hold values from 0.099609375 to 1.8984375
- ln1_bias: bfloat16 [768], replicated, may hold values from -3 to 3
- w_in: bfloat16 [768, 3072], P(None, 'mp'), may hold values from -0.21875 to 0.21875
- b_in: bfloat16 [3072], P('mp'), may hold values from -3 to 3
- w_out: bfloat16 [3072, 768], P('mp'), may hold values from -0.21875 to 0.21875
- b_out: bfloat16 [768], replicated, may hold values from -3 to 3
- ln2_gain: bfloat16 [768], replicated, may hold values from 0.099609375 to 1.8984375
- ln2_bias: bfloat16 [768], replicated, may hold values from -3 to 3
- grad_out: bfloat16 [32768, 768], P(('dp', 'mp')), may hold values from -6 to 6
Outputs:
- output: bfloat16 [32768, 768], P(('dp', 'mp'))
- grad_tokens: float32 [32768, 768], P(('dp', 'mp'))
- grad_ln1_gain: float32 [768], replicated
- grad_ln1_bias: float32 [768], replicated
- grad_w_in: float32 [768, 3072], P(None, 'mp')
- grad_b_in: float32 [3072], P('mp')
- grad_w_out: float32 [3072, 768], P('mp')
- grad_b_out: float32 [768], replicated
- grad_ln2_gain: float32 [768], replicated
- grad_ln2_bias: float32 [768], replicated
The draws below stay inside these ranges and needn't reach their ends.
Inputs may be any that keep to these rules, and one draw needn't show every extreme that they name: The sequences of block b have 512 // 2 ** block_kind[b] tokens each and fill the block.
All inputs are finite; a program needn't handle non-finite values.
Results may differ from the reference program's by a relative error of at most 0.0095.
Values may be sent and summed in bfloat16 or wider, within the bound.
A program may use at most 128 MiB of HBM per device.

```python
import math
import jax
import jax.numpy as jnp
from jax import lax

D = 768
FF = 3072
BLOCK = 512
BLK_DEV = 2
BLOCKS = 64
TOKENS = 32768
N_DP = 8
N_MP = 4


def touch_ends(entries, rng, smallest, largest):
    spot = [jax.random.randint(jax.random.fold_in(rng, axis), (), 0, length) for axis, length in enumerate(entries.shape)]
    longest = entries.shape.index(max(entries.shape))
    next_to = spot[:longest] + [(spot[longest] + 1) % entries.shape[longest]] + spot[longest + 1:]
    return entries.at[tuple(spot)].set(smallest).at[tuple(next_to)].set(largest)


def block_scale(own_key, shape, split, least, top_value):
    level = 1.0
    for position, blocks in split:
        draws = jax.random.uniform(jax.random.fold_in(jax.random.fold_in(own_key, 6), position), (blocks,), jnp.float32, least / len(split), top_value / len(split))
        level = level * jnp.repeat(jnp.exp(draws), shape[position] // blocks).reshape((-1,) + (1,) * (len(shape) - 1 - position))
    return level


def noise(own_key, shape, deviation, bound, pieces=(), kind=jnp.bfloat16):
    result = jax.random.normal(own_key, shape, jnp.float32) * deviation
    if len(pieces) > 0:
        result = block_scale(own_key, shape, pieces, -0.22, 0.18) * result
    return jnp.clip(result, min=-bound, max=bound).astype(kind)


def setup_inputs(seed: int = 0) -> dict:
    streams_of = jax.random.split(jax.random.key(seed), 12)
    tokens = noise(streams_of[0], (TOKENS, D), 1.0, 6.0, ((0, 32),))
    block_kind = touch_ends(jax.random.randint(streams_of[1], (BLOCKS,), 0, 3), jax.random.fold_in(streams_of[1], 1), 0, 2).astype(jnp.int32)
    ln1_gain = jnp.clip(1.0 + 0.18 * jax.random.normal(streams_of[2], (D,), jnp.float32), 0.099609375, 1.8984375).astype(jnp.bfloat16)
    ln1_bias = noise(streams_of[3], (D,), 0.5, 3.0)
    w_in = noise(streams_of[4], (D, FF), D ** -0.5, 0.21875, ((1, 4),))
    b_in = noise(streams_of[5], (FF,), 0.5, 3.0, ((0, 4),))
    w_out = noise(streams_of[6], (FF, D), (FF // 4) ** -0.5, 0.21875, ((0, 4),))
    b_out = noise(streams_of[7], (D,), 0.5, 3.0)
    ln2_gain = jnp.clip(1.0 + 0.18 * jax.random.normal(streams_of[8], (D,), jnp.float32), 0.099609375, 1.8984375).astype(jnp.bfloat16)
    ln2_bias = noise(streams_of[9], (D,), 0.5, 3.0)
    grad_out = noise(streams_of[10], (TOKENS, D), 1.0, 6.0, ((0, 32),))
    return dict(tokens=tokens, block_kind=block_kind, ln1_gain=ln1_gain, ln1_bias=ln1_bias, w_in=w_in, b_in=b_in, w_out=w_out, b_out=b_out, ln2_gain=ln2_gain, ln2_bias=ln2_bias, grad_out=grad_out)


@jax.custom_vjp
def low(v):
    return lax.optimization_barrier(v.astype(jnp.bfloat16)).astype(jnp.float32)

@jax.custom_vjp
def low_back(v):
    return v

def low_keep(v):
    return (low(v), None)

def low_pass(kept, grad):
    return (grad,)

def back_keep(v):
    return (v, None)

def back_low(kept, grad):
    return (low(grad),)
low.defvjp(low_keep, low_pass)
low_back.defvjp(back_keep, back_low)

def rounded_table(values):
    return lax.optimization_barrier(values.astype(jnp.bfloat16)).astype(jnp.float32)

def sequence_tables(block_len):
    row_ids = jnp.arange(block_len, dtype=jnp.int32)
    cosines = []
    sines = []
    for variant in range(3):
        seq_len = block_len // 2 ** variant
        places = row_ids % seq_len
        owners = row_ids // seq_len
        same_seq = owners[:, None] == owners[None, :]
        phase = places[:, None] * places[None, :] % seq_len
        angle = phase.astype(jnp.float32) * (2.0 * math.pi / seq_len)
        factor = 1.0 / math.sqrt(seq_len)
        cosines.append(jnp.where(same_seq, jnp.cos(angle) * factor, 0.0))
        sines.append(jnp.where(same_seq, jnp.sin(angle) * factor, 0.0))
    return (jnp.stack(cosines), jnp.stack(sines))

def width_tables(count):
    row_ids = jnp.arange(count, dtype=jnp.int32)
    phase = row_ids[:, None] * row_ids[None, :] % count
    angle = phase.astype(jnp.float32) * (2.0 * math.pi / count)
    factor = 1.0 / math.sqrt(count)
    return (jnp.cos(angle) * factor, jnp.sin(angle) * factor)

def layer_norm(values, gain, shift):
    centre = values - lax.optimization_barrier(jnp.mean(values, axis=-1, keepdims=True))
    spread = lax.optimization_barrier(jnp.mean(centre * centre, axis=-1, keepdims=True))
    return centre * lax.rsqrt(spread + 1e-05) * gain + shift

def group_forward(params, tables, inputs):
    gain_one, shift_one, weight_in, bias_in, weight_out, bias_out, gain_two, shift_two = params
    cos_seq, sin_seq, cos_feat, sin_feat = tables
    rows_grp, variants = inputs
    seq_cos = cos_seq[variants]
    seq_sin = sin_seq[variants]
    highest = lax.Precision.HIGHEST
    by_cos = low_back(low(jnp.einsum('bsd,de->bse', rows_grp, cos_feat, precision=highest)))
    by_sin = low_back(low(jnp.einsum('bsd,de->bse', rows_grp, sin_feat, precision=highest)))
    mixed = jnp.einsum('bst,btd->bsd', seq_cos, by_cos, precision=highest) - jnp.einsum('bst,btd->bsd', seq_sin, by_sin, precision=highest)
    mixed = low_back(mixed)
    normed = layer_norm(rows_grp + mixed, gain_one, shift_one)
    normed_low = low(normed)
    hidden_pre = low_back(jnp.einsum('bsd,df->bsf', normed_low, weight_in, precision=highest) + bias_in)
    hidden_low = low(jax.nn.gelu(hidden_pre, approximate=True))
    branch = low_back(jnp.einsum('bsf,fd->bsd', hidden_low, weight_out, precision=highest) + bias_out)
    return layer_norm(normed + branch, gain_two, shift_two)

def reference(tokens, block_kind, ln1_gain, ln1_bias, w_in, b_in, w_out, b_out, ln2_gain, ln2_bias, grad_out):
    cos_seq, sin_seq = sequence_tables(BLOCK)
    cos_feat, sin_feat = width_tables(D)
    tables = (rounded_table(cos_seq), rounded_table(sin_seq), rounded_table(cos_feat), rounded_table(sin_feat))
    params = tuple((p.astype(jnp.float32) for p in (ln1_gain, ln1_bias, w_in, b_in, w_out, b_out, ln2_gain, ln2_bias)))
    groups = N_DP
    per_group = BLK_DEV * N_MP
    kinds_grp = block_kind.astype(jnp.int32).reshape(groups, per_group)

    def forward(weights, inputs):
        shaped = inputs.reshape(groups, per_group, BLOCK, D)

        def group_step(pair_in):
            return group_forward(weights, tables, pair_in)
        results = lax.map(jax.checkpoint(group_step), (shaped, kinds_grp))
        return results.reshape(TOKENS, D)
    output, pullback = jax.vjp(forward, params, tokens.astype(jnp.float32))
    param_grads, input_grad = pullback(grad_out.astype(jnp.float32))
    return (output.astype(jnp.bfloat16), input_grad, param_grads[0], param_grads[1], param_grads[2], param_grads[3], param_grads[4], param_grads[5], param_grads[6], param_grads[7])
```

```python
import functools
import math

import jax
import jax.numpy as jnp
import numpy as np
from jax import lax
from jax.experimental import pallas as pl
from jax.experimental.pallas import tpu as pltpu
from jax.sharding import PartitionSpec as P

BLOCK = 512
NT = 256
RT = 128
F32 = jnp.float32
BF16 = jnp.bfloat16
SQRT_2_PI = math.sqrt(2.0 / math.pi)


def sequence_table():
    ids = np.arange(BLOCK)
    out = []
    for variant in range(3):
        n = BLOCK // 2**variant
        place, owner = ids % n, ids // n
        same = owner[:, None] == owner[None, :]
        angle = (place[:, None] * place[None, :] % n) * (2.0 * math.pi / n)
        factor = 1.0 / math.sqrt(n)
        cos = np.where(same, np.cos(angle) * factor, 0.0)
        sin = np.where(same, np.sin(angle) * factor, 0.0)
        out.append(np.concatenate([cos, -sin], axis=1))
    return np.stack(out).astype(np.float32).astype(BF16)


def feature_table(n):
    ids = np.arange(n)
    angle = (ids[:, None] * ids[None, :] % n) * (2.0 * math.pi / n)
    factor = 1.0 / math.sqrt(n)
    return np.concatenate([np.cos(angle), np.sin(angle)], axis=1).astype(np.float32).__mul__(np.float32(factor)).astype(BF16)


def mm(a, b):
    return lax.dot_general(a, b, (((1,), (0,)), ((), ())), preferred_element_type=F32)


def mm_t(a, b):
    return lax.dot_general(a, b, (((1,), (1,)), ((), ())), preferred_element_type=F32)


def fold(v):
    return jnp.sum(v.reshape(v.shape[0] // 8, 8, v.shape[1]), axis=0)


def gelu_both(v):
    sq = v * v
    t = jnp.tanh(SQRT_2_PI * v * (1.0 + 0.044715 * sq))
    u = 0.5 * (1.0 + t)
    slope = u + (0.5 * SQRT_2_PI) * v * (1.0 - t * t) * (1.0 + (3 * 0.044715) * sq)
    return v * u, slope


def layer_kernel(
    kind, vecs, b_in, tok_hbm, go_hbm, feat_hbm, seq_hbm, win_hbm, wout_hbm,
    out_hbm, gt_hbm, dwin_hbm, dwout_hbm, vec_out,
    tok, go, feat, seq, win, wout, hid, slope, xhat, acc, x, xt, g, gt, by, rstd, part, sems,
):
    rows, width = tok.shape
    shards = win.shape[0]
    hidden = win.shape[2]
    blocks = rows // BLOCK
    loads = [
        pltpu.make_async_copy(src, dst, sems.at[i])
        for i, (src, dst) in enumerate(
            [(tok_hbm, tok), (feat_hbm, feat), (seq_hbm, seq), (win_hbm, win), (wout_hbm, wout), (go_hbm, go)]
        )
    ]
    for c in loads:
        c.start()
    loads[0].wait()
    loads[1].wait()
    g1, s1, bo, g2, s2 = (vecs[i : i + 1, :] for i in range(5))
    tiles = [slice(i * NT, (i + 1) * NT) for i in range(width // NT)]
    htiles = [slice(i * NT, (i + 1) * NT) for i in range(hidden // NT)]

    for b in range(blocks):
        r = slice(b * BLOCK, (b + 1) * BLOCK)
        for c in tiles:
            by[0:BLOCK, c] = mm(tok[r, :], feat[:, c]).astype(BF16)
            c2 = slice(c.start + width, c.stop + width)
            by[BLOCK:, c] = mm(tok[r, :], feat[:, c2]).astype(BF16)
        if b == 0:
            loads[2].wait()
        k = kind[b]
        for c in tiles:
            xhat[r, c] = tok[r, c].astype(F32) + mm(seq[k], by[:, c])

        def norm_one(i, _, b=b):
            q = pl.ds(pl.multiple_of(b * BLOCK + i * RT, RT), RT)
            v = xhat[q, :]
            centre = v - jnp.mean(v, axis=-1, keepdims=True)
            rs = lax.rsqrt(jnp.mean(centre * centre, axis=-1, keepdims=True) + 1e-5)
            h = centre * rs
            xhat[q, :] = h
            rstd[q, :] = rs
            x[q, :] = (h * g1 + s1).astype(BF16)
            return 0

        lax.fori_loop(0, BLOCK // RT, norm_one, 0)
        for c in tiles:
            xt[c, r] = x[r, c].T

    loads[3].wait()
    loads[4].wait()

    def forward(s, _):
        for c in htiles:
            pre = mm(x[...], win[s, :, c]) + b_in[pl.ds(s, 1), c]
            a, d = gelu_both(pre)
            hid[s, :, c] = a.astype(BF16)
            slope[s, :, c] = d.astype(BF16)
        for c in tiles:
            acc[:, c] = acc[:, c] + mm(hid[s], wout[s, :, c])
        return 0

    acc[...] = jnp.zeros_like(acc)
    lax.fori_loop(0, shards, forward, 0)
    loads[5].wait()

    def norm_two(i, sums):
        q = pl.ds(pl.multiple_of(i * RT, RT), RT)
        v = xhat[q, :] * g1 + s1 + (acc[q, :] + bo)
        centre = v - jnp.mean(v, axis=-1, keepdims=True)
        rs = lax.rsqrt(jnp.mean(centre * centre, axis=-1, keepdims=True) + 1e-5)
        h = centre * rs
        tok[q, :] = (h * g2 + s2).astype(BF16)
        cot = go[q, :].astype(F32)
        dh = cot * g2
        gr = rs * (dh - jnp.mean(dh, axis=-1, keepdims=True) - h * jnp.mean(dh * h, axis=-1, keepdims=True))
        acc[q, :] = gr
        low = gr.astype(BF16)
        g[q, :] = low
        return (sums[0] + fold(cot * h), sums[1] + fold(cot), sums[2] + fold(low.astype(F32)))

    zero = jnp.zeros((8, width), F32)
    dg2, ds2, dbo = lax.fori_loop(0, rows // RT, norm_two, (zero, zero, zero))
    put_out = pltpu.make_async_copy(tok, out_hbm, sems.at[0])
    put_out.start()
    part[0:8, :] = dg2
    part[8:16, :] = ds2
    part[16:24, :] = dbo
    for b in range(blocks):
        r = slice(b * BLOCK, (b + 1) * BLOCK)
        for c in tiles:
            gt[c, r] = g[r, c].T

    def backward(s, _):
        for c in htiles:
            dwout_v[s, :, c] = mm(gt[...], hid[s, :, c]).astype(BF16)
        for c in htiles:
            gp = (mm_t(g[...], wout[s, c, :]) * slope[s, :, c].astype(F32)).astype(BF16)
            slope[s, :, c] = gp
            vec_out[pl.ds(5 + s, 1), c] = jnp.sum(fold(gp.astype(F32)), axis=0, keepdims=True)
        for c in htiles:
            dwin_v[s, :, c] = mm(xt[...], slope[s, :, c]).astype(BF16)
        return 0

    dwout_v, dwin_v = dwout_hbm, dwin_hbm
    vec_out[...] = jnp.zeros_like(vec_out)
    lax.fori_loop(0, shards, backward, 0)

    for c in tiles:
        total = acc[:, c]
        for s in range(shards):
            total = total + mm_t(slope[s], win[s, c, :])
        acc[:, c] = total

    put_out.wait()

    def back_one(i, sums):
        q = pl.ds(pl.multiple_of(i * RT, RT), RT)
        gn = acc[q, :]
        h = xhat[q, :]
        dh = gn * g1
        gs = rstd[q, :] * (dh - jnp.mean(dh, axis=-1, keepdims=True) - h * jnp.mean(dh * h, axis=-1, keepdims=True))
        acc[q, :] = gs
        tok[q, :] = gs.astype(BF16)
        return (sums[0] + fold(gn * h), sums[1] + fold(gn))

    dg1, ds1 = lax.fori_loop(0, rows // RT, back_one, (zero, zero))
    for i, v in enumerate((dg1, ds1, dbo, dg2, ds2)):
        vec_out[i : i + 1, :] = jnp.sum(v, axis=0, keepdims=True)
    for b in range(blocks):
        r = slice(b * BLOCK, (b + 1) * BLOCK)
        k = kind[b]
        for c in tiles:
            by[0:BLOCK, c] = mm(seq[k, :, 0:BLOCK], tok[r, c]).astype(BF16)
            by[BLOCK:, c] = mm(seq[k, :, BLOCK:], tok[r, c]).astype(BF16)
        for c in tiles:
            c2 = slice(c.start + width, c.stop + width)
            acc[r, c] = acc[r, c] + mm(by[0:BLOCK, :], feat[:, c]) + mm(by[BLOCK:, :], feat[:, c2])
    put = pltpu.make_async_copy(acc, gt_hbm, sems.at[0])
    put.start()
    put.wait()


def layer(kind, vecs, b_in, tokens, grad_out, feat, seq, win, wout):
    rows, width = tokens.shape
    shards, _, hidden = win.shape
    any_spec = pl.BlockSpec(memory_space=pl.ANY)
    vmem = pl.BlockSpec(memory_space=pltpu.VMEM)
    dw = jax.ShapeDtypeStruct((shards, width, hidden), BF16)
    return pl.pallas_call(
        layer_kernel,
        out_shape=(
            jax.ShapeDtypeStruct((rows, width), BF16),
            jax.ShapeDtypeStruct((rows, width), F32),
            dw,
            dw,
            jax.ShapeDtypeStruct((16, width), F32),
        ),
        in_specs=[pl.BlockSpec(memory_space=pltpu.SMEM), vmem, vmem] + [any_spec] * 6,
        out_specs=[any_spec, any_spec, vmem, vmem, vmem],
        scratch_shapes=[
            pltpu.VMEM((rows, width), BF16),
            pltpu.VMEM((rows, width), BF16),
            pltpu.VMEM(feat.shape, BF16),
            pltpu.VMEM(seq.shape, BF16),
            pltpu.VMEM(win.shape, BF16),
            pltpu.VMEM(wout.shape, BF16),
            pltpu.VMEM((shards, rows, hidden), BF16),
            pltpu.VMEM((shards, rows, hidden), BF16),
            pltpu.VMEM((rows, width), F32),
            pltpu.VMEM((rows, width), F32),
            pltpu.VMEM((rows, width), BF16),
            pltpu.VMEM((width, rows), BF16),
            pltpu.VMEM((rows, width), BF16),
            pltpu.VMEM((width, rows), BF16),
            pltpu.VMEM((2 * BLOCK, width), BF16),
            pltpu.VMEM((rows, 1), F32),
            pltpu.VMEM((24, width), F32),
            pltpu.SemaphoreType.DMA((6,)),
        ],
        compiler_params=pltpu.CompilerParams(vmem_limit_bytes=63 * 2**20),
    )(kind, vecs, b_in, tokens, grad_out, feat, seq, win, wout)


def local(
    tokens, block_kind, ln1_gain, ln1_bias, w_in, b_in, w_out, b_out, ln2_gain, ln2_bias, grad_out
):
    n_dp, n_mp = lax.axis_size("dp"), lax.axis_size("mp")
    both = ("mp", "dp")
    width, hidden = w_in.shape
    vecs = jnp.stack([ln1_gain, ln1_bias, b_out, ln2_gain, ln2_bias]).astype(F32)
    vecs = jnp.pad(vecs, ((0, 3), (0, 0)))
    bias = lax.all_gather(b_in, "mp").astype(F32)
    d = lax.axis_index("dp")
    part = width // n_dp
    mine = jnp.stack(
        [lax.dynamic_slice_in_dim(w_in, d * part, part), lax.dynamic_slice_in_dim(w_out, d * part, part)]
    )
    full = lax.all_gather(mine, both).reshape(n_mp, n_dp, 2, part, hidden)
    full = full.transpose(2, 0, 1, 3, 4).reshape(2, n_mp, width, hidden)
    feat = jnp.asarray(feature_table(width))
    seq = jnp.asarray(sequence_table())
    out, gt, dwin, dwout, vec = layer(
        block_kind, vecs, bias, tokens, grad_out, feat, seq, full[0], full[1]
    )
    dws = jnp.stack([dwin, dwout], axis=2).reshape(n_mp * width * 2, hidden)
    dws = lax.psum_scatter(dws, both, scatter_dimension=0, tiled=True)
    dws = lax.all_gather(dws, "dp", axis=0, tiled=True).reshape(width, 2, hidden)
    small = lax.psum(vec, ("dp", "mp"))
    grad_b_in = lax.dynamic_index_in_dim(small, 5 + lax.axis_index("mp"), 0, keepdims=False)
    return (
        out,
        gt,
        small[0],
        small[1],
        dws[:, 0].astype(F32),
        grad_b_in,
        dws[:, 1].astype(F32).T,
        small[2],
        small[3],
        small[4],
    )


def solution(mesh):
    in_specs = (
        P(("dp", "mp"), None),
        P(("dp", "mp")),
        P(),
        P(),
        P(None, "mp"),
        P("mp"),
        P("mp", None),
        P(),
        P(),
        P(),
        P(("dp", "mp"), None),
    )
    out_specs = (
        P(("dp", "mp"), None),
        P(("dp", "mp"), None),
        P(),
        P(),
        P(None, "mp"),
        P("mp"),
        P("mp", None),
        P(),
        P(),
        P(),
    )
    return jax.shard_map(local, mesh=mesh, in_specs=in_specs, out_specs=out_specs, check_vma=False)
```

```python
import functools
import math

import jax
import jax.numpy as jnp
import numpy as np
from jax import lax
from jax.experimental import pallas as pl
from jax.experimental.pallas import tpu as pltpu
from jax.sharding import PartitionSpec as P

BLOCK = 512
NT = 256
RT = 256
VMEM_LIMIT = 64 * 2**20 - 2**18
F32 = jnp.float32
BF16 = jnp.bfloat16
SQRT_2_PI = math.sqrt(2.0 / math.pi)


def sequence_table():
    ids = np.arange(BLOCK)
    out = []
    for variant in range(3):
        n = BLOCK // 2**variant
        place, owner = ids % n, ids // n
        same = owner[:, None] == owner[None, :]
        angle = (place[:, None] * place[None, :] % n) * (2.0 * math.pi / n)
        factor = 1.0 / math.sqrt(n)
        cos = np.where(same, np.cos(angle) * factor, 0.0)
        sin = np.where(same, np.sin(angle) * factor, 0.0)
        out.append(np.concatenate([cos, -sin], axis=1))
    return np.stack(out).astype(np.float32).astype(BF16)


def feature_table(n):
    ids = np.arange(n)
    angle = (ids[:, None] * ids[None, :] % n) * (2.0 * math.pi / n)
    factor = 1.0 / math.sqrt(n)
    return np.concatenate([np.cos(angle), np.sin(angle)], axis=1).astype(np.float32).__mul__(np.float32(factor)).astype(BF16)


def mm(a, b):
    return lax.dot_general(a, b, (((1,), (0,)), ((), ())), preferred_element_type=F32)


def mm_t(a, b):
    return lax.dot_general(a, b, (((1,), (1,)), ((), ())), preferred_element_type=F32)


def fold(v):
    return jnp.sum(v.reshape(v.shape[0] // 8, 8, v.shape[1]), axis=0)


def gelu_both(v):
    sq = v * v
    t = jnp.tanh(SQRT_2_PI * v * (1.0 + 0.044715 * sq))
    u = 0.5 * (1.0 + t)
    slope = u + (0.5 * SQRT_2_PI) * v * (1.0 - t * t) * (1.0 + (3 * 0.044715) * sq)
    return v * u, slope

MESH = pl.DeviceIdType.MESH
GROUP = 8

PARTS = 2
SPLIT = 2

FORWARD = (
    "INIT Ma.0 Mb.0 E1.0.0.0",
    "Mc.0 E1.0.0.1 Ma.1 E1.0.1.0",
    "E2.0.0.0 E1.1.0.1 DG.1.0 Mb.1",
    "E2.0.0.1 Mc.1 E1.1.0.0 DG.1.1",
    "A.0.0 E1.0.1.1 A.0.1 A.0.2",
    "E3.0.0.0 B.0.0 E1.2.0.1 E2.1.0.1",
    "E2.0.1.0 B.0.1 E3.0.0.1 B.0.2",
    "DF.0.1.0 E2.1.0.0 E1.2.0.0 E3.0.1.0",
    "E4.0.0 A.1.0 E1.1.1.1 A.1.1",
    "DF.0.1.1 E2.1.1.1 E2.0.1.1 E3.0.1.1",
    "A.1.2 E1.1.1.0 E2.2.0.1 E4.0.1",
    "B.1.0 E3.1.0.0 DF.1.1.1 E3.1.0.1",
    "B.1.1 B.1.2 E2.2.0.0 E1.2.1.1",
    "E4.1.0 A.2.0 DF.1.1.0 A.2.1",
    "E2.1.1.0 E3.1.1.1 A.2.2 E3.1.1.0",
    "E1.2.1.0 E2.2.1.0 DF.2.1.1 DF.2.1.0",
    "E3.2.0.1 E3.2.0.0 E2.2.1.1 E4.1.1",
    "B.2.0 B.2.1 B.2.2 E3.2.1.1",
    "E4.2.0 A.3.0 E3.2.1.0 A.3.1",
    "A.3.2 E4.2.1 B.3.0 B.3.1",
    "B.3.2 N2",
)
BACKWARD = (
    "Oa.0 Oa.1 Ob.0 U1.0.0.1",
    "Oa.2 U1.0.0.0 G.3.0 Ob.1",
    "G.0.0 U2.0.0.1 U1.1.0.0 Oa.3",
    "U1.1.0.1 Ob.2 U2.0.0.0 G.0.1",
    "U1.2.0.0 Ob.3 G.0.2 U1.3.0.1",
    "U3.0.0.1 U2.1.0.0 Ia.0 U1.2.0.1",
    "U2.2.0.0 Ib.0 U1.0.1.0 U3.0.0.0",
    "G.1.0 G.1.1 U1.0.1.1 U1.3.0.0",
    "G.1.2 Ia.1 U3.2.0.0 U2.1.0.1",
    "U3.1.0.1 Ib.1 G.2.0 U3.1.0.0",
    "U1.1.1.1 G.2.1 G.2.2 U1.1.1.0",
    "Ia.2 U2.0.1.0 Ib.2 U2.2.0.1",
    "U1.2.1.0 U3.2.0.1 G.3.1 G.3.2",
    "U1.2.1.1 Ia.3 U2.0.1.1 Ib.3",
    "U2.1.1.0 U1.3.1.0 U3.0.1.0 U2.1.1.1",
    "U1.3.1.1 X.0 U2.3.0.0 U3.3.0.0",
    "X.1 U3.0.1.1 U3.1.1.0 U2.3.0.1",
    "U3.3.0.1 X.2 U2.2.1.0 U3.2.1.0",
    "F2.3.0.0 N1.0 N1.1 V.0",
    "U3.1.1.1 U2.2.1.1 U3.2.1.1 V.1",
    "F2.3.0.1 F3.3.0.0 U2.3.1.1 Q.0",
    "U2.3.1.0 V.2 U3.3.1.0 R.0",
    "U3.3.1.1 V.3 F3.3.0.1 F2.3.1.0",
    "Q.1 F2.3.1.1 R.1 F3.3.1.0",
    "F4.3.0 F3.3.1.1 V.4 F4.3.1",
)

def pick(i, table):
    n = len(table)
    total = jnp.int32(0)
    for k, v in enumerate(table):
        total = total + v * (1 - lax.div(lax.rem(i - k + n, n) + (n - 1), n))
    return total


def layer_kernel(
    n, kind, g1_ref, s1_ref, bo_ref, g2_ref, s2_ref, bin_ref, tok_hbm, go_hbm, feat_hbm, seq_hbm, win_hbm, wout_hbm,
    out_hbm, gt_hbm, dwin_hbm, dwout_hbm, vec_out,
    tok, feat, seq, win, wout, hid, slope, xhat, acc, xg, xt, gt, by, rstd, bias, part,
    pout, r0, rxy, rz, rf, fin, va, vr, vz,
    load_sem, sent, zs, zr, dr, xr, yr, xyr, fr, cr, hr, tr, ur, far, fbr, fcr, vrr, once,
):
    rows, width = tok.shape
    hidden = win.shape[2]
    blocks = rows // BLOCK
    weights = (win, wout)
    d, m = lax.axis_index("dp"), lax.axis_index("mp")
    core, xx, yy = lax.rem(d, 2), lax.rem(lax.div(d, 2), 2), lax.rem(lax.div(d, 4), 2)
    to_core, to_x, to_y = (d + 1 - 2 * core, m), (d + 2 - 4 * xx, m), (d + 4 - 8 * yy, m)
    others = [(d, lax.rem(m + t, n)) for t in range(1, n)]
    up, down = (d, m + 1), (d, m - 1)
    foreign_order = [sorted((s for s in range(n) if s != mm), key=lambda s: (abs(s - mm), s)) for mm in range(n)]
    far_order = [sorted(range(n), key=lambda s: (-abs(s - mm), abs(2 * s - n + 1) * -1)) for mm in range(n)]
    foreign = [pick(m, [foreign_order[mm][k] for mm in range(n)]) for k in range(n - 1)]
    target = [pick(m, [far_order[mm][k] for mm in range(n)]) for k in range(n)]
    tiles = [slice(i * NT, (i + 1) * NT) for i in range(width // NT)]
    htiles = [slice(i * NT, (i + 1) * NT) for i in range(hidden // NT)]
    half = width // 2
    piece = half // (4 * PARTS)
    s_xy, s_f, s_c, s_h, s_t, s_u, s_fa, s_fc, s_b, s_v, s_vz = (sent.at[i] for i in range(11))

    def remote(src, dst, ssem, rsem, dev):
        return pltpu.make_async_remote_copy(
            src_ref=src, dst_ref=dst, send_sem=ssem, recv_sem=rsem, device_id=dev, device_id_type=MESH
        )

    def send(src, dst, ssem, rsem, dev, cond=None):
        copy = remote(src, dst, ssem, rsem, dev)
        if cond is None:
            copy.start()
        else:
            pl.when(cond)(copy.start)

    def all_sent(ref, sem):
        remote(ref, ref, sem, sem, to_core).wait_send()

    def arrived(dst, rsem):
        remote(dst, dst, rsem, rsem, to_core).wait_recv()

    barrier = pltpu.get_barrier_semaphore()
    partners = [to_core, to_x, to_y] + others
    for dev in partners:
        pl.semaphore_signal(barrier, inc=1, device_id=dev, device_id_type=MESH)
    loads = [
        pltpu.make_async_copy(a, b, load_sem.at[i])
        for i, (a, b) in enumerate(
            [(tok_hbm, tok), (feat_hbm, feat), (seq_hbm, seq), (win_hbm, win.at[m]), (wout_hbm, wout.at[m]), (go_hbm, by)]
        )
    ]
    for c in loads[:5]:
        c.start()
    g1, s1, bo, g2, s2 = (
        r[...].astype(F32).reshape(1, width) for r in (g1_ref, s1_ref, bo_ref, g2_ref, s2_ref)
    )
    bias[pl.ds(m, 1)] = jnp.broadcast_to(bin_ref[...].astype(F32).reshape(1, 1, hidden), (1, 8, hidden))
    pl.semaphore_wait(barrier, len(partners))

    def span(start, size):
        return pl.ds(pl.multiple_of(start, 16), size)

    mine, by_x, by_y, diag = 2 * yy + xx, 2 * yy + (1 - xx), 2 * (1 - yy) + xx, 2 * (1 - yy) + (1 - xx)

    def rows_of(w, h, q):
        size = w.shape[0] // (GROUP * PARTS)
        return span(((core * PARTS + h) * 4 + q) * size, size)

    def wblock(i, s, h, q):
        return weights[i].at[s, rows_of(weights[i].at[0], h, q)]

    def wpart(i, s, h, c):
        size = weights[i].shape[1] // (2 * PARTS)
        return weights[i].at[s, span((c * PARTS + h) * size, size)]

    def along(s, src, dst, rsem):
        send(src, dst, zs.at[0, s], rsem, up, (s <= m) & (m < n - 1))
        send(src, dst, zs.at[1, s], rsem, down, (s >= m) & (m > 0))

    def init():
        for i, w in enumerate((win_hbm, wout_hbm)):
            for h in range(PARTS):
                along(m, w.at[rows_of(w, h, mine)], wblock(i, m, h, mine), zr.at[i, h, m])
            if i == 0:
                for dev in others:
                    send(bias.at[m], bias.at[m], s_b, once.at[0], dev)

    def dg(i, h):
        w = (win_hbm, wout_hbm)[i]
        along(m, w.at[rows_of(w, h, diag)], wblock(i, m, h, diag), dr.at[h, m])

    def df(k, i, h):
        s = foreign[k]
        block = wblock(i, s, h, diag)

        @pl.when(((s < m) & (m < n - 1)) | ((s > m) & (m > 0)))
        def _():
            arrived(block, dr.at[h, s])

        along(s, block, block, dr.at[h, s])

    def e1(k, i, h):
        s = foreign[k]
        block = wblock(i, s, h, mine)
        arrived(block, zr.at[i, h, s])
        send(block, block, s_xy, (xr, xyr)[i].at[k, h], to_x)
        send(block, block, s_xy, (yr, xyr)[i].at[k, h], to_y)
        along(s, block, block, zr.at[i, h, s])

    def e2(k, i, h):
        s = foreign[k]
        if i == 1:
            return
        if h % 2 == 0:
            block = wblock(i, s, h, by_x)
            arrived(block, xr.at[k, h])
            send(block, block, s_f, fr.at[k, h], to_y)
        else:
            block = wblock(i, s, h, by_y)
            arrived(block, yr.at[k, h])
            send(block, block, s_f, fr.at[k, h], to_x)

    def e3(k, i, h):
        s = foreign[k]
        if i == 0:
            if h % 2 == 0:
                arrived(wblock(i, s, h, by_y), yr.at[k, h])
            else:
                arrived(wblock(i, s, h, by_x), xr.at[k, h])
            arrived(wblock(i, s, h, diag), fr.at[k, h])
        else:
            arrived(wout.at[s, pl.ds(0, 2 * piece)], xyr.at[k, h])
            at_edge = ((s < m) & (m == n - 1)) | ((s > m) & (m == 0))

            @pl.when(at_edge)
            def _():
                arrived(wblock(i, s, h, diag), dr.at[h, s])

        block = wpart(i, s, h, core)
        send(block, block, s_c, cr.at[k, i], to_core)

    def e4(k, i):
        s = foreign[k]
        arrived(weights[i].at[s, span((1 - core) * half, half)], cr.at[k, i])
        if i == 0 and k == 0:
            arrived(bias.at[pl.ds(0, n - 1)], once.at[0])

    def mix_feat(b):
        if b == 0:
            loads[0].wait()
            loads[1].wait()
        r = slice(b * BLOCK, (b + 1) * BLOCK)
        for c in tiles:
            by[0:BLOCK, c] = mm(tok[r, :], feat[:, c]).astype(BF16)
            c2 = slice(c.start + width, c.stop + width)
            by[BLOCK : 2 * BLOCK, c] = mm(tok[r, :], feat[:, c2]).astype(BF16)

    def mix_seq(b):
        if b == 0:
            loads[2].wait()
        r = slice(b * BLOCK, (b + 1) * BLOCK)
        k = kind[b]
        for c in tiles:
            xhat[r, c] = tok[r, c].astype(F32) + mm(seq[k], by[:, c])

    def mix_norm(b):
        r = slice(b * BLOCK, (b + 1) * BLOCK)

        def norm_one(i, _):
            q = pl.ds(pl.multiple_of(b * BLOCK + i * RT, RT), RT)
            v = xhat[q, :]
            centre = v - jnp.mean(v, axis=-1, keepdims=True)
            rs = lax.rsqrt(jnp.mean(centre * centre, axis=-1, keepdims=True) + 1e-5)
            h = centre * rs
            xhat[q, :] = h
            rstd[q, :] = rs
            xg[q, :] = (h * g1 + s1).astype(BF16)
            return 0

        lax.fori_loop(0, BLOCK // RT, norm_one, 0)
        for c in tiles:
            xt[c, r] = xg[r, c].T
        if b == blocks - 1:
            loads[5].start()

    def fwd_a(f, t):
        if f == 0 and t == 0:
            loads[3].wait()
        s = m if f == 0 else foreign[f - 1]
        c = htiles[t]
        pre = mm(xg[...], win[s, :, c]) + bias[s, 0:1, c]
        a, dv = gelu_both(pre)
        hid[s, :, c] = a.astype(BF16)
        slope[s, :, c] = dv.astype(BF16)

    def fwd_b(f, t):
        if f == 0 and t == 0:
            loads[4].wait()
        s = m if f == 0 else foreign[f - 1]
        c = tiles[t]
        term = mm(hid[s], wout[s, :, c])
        acc[:, c] = term if f == 0 else acc[:, c] + term

    zero = jnp.zeros((8, width), F32)
    put_out = pltpu.make_async_copy(tok, out_hbm, load_sem.at[0])
    put_gt = pltpu.make_async_copy(acc, gt_hbm, load_sem.at[1])
    put_win = pltpu.make_async_copy(fin.at[1], dwin_hbm, load_sem.at[2])
    put_wout = pltpu.make_async_copy(xg.at[pl.ds(0, hidden)], dwout_hbm, load_sem.at[3])

    def norm_two():
        loads[5].wait()

        def step(i, sums):
            q = pl.ds(pl.multiple_of(i * RT, RT), RT)
            v = xhat[q, :] * g1 + s1 + (acc[q, :] + bo)
            centre = v - jnp.mean(v, axis=-1, keepdims=True)
            rs = lax.rsqrt(jnp.mean(centre * centre, axis=-1, keepdims=True) + 1e-5)
            h = centre * rs
            tok[q, :] = (h * g2 + s2).astype(BF16)
            cot = by[q, :].astype(F32)
            dh = cot * g2
            gr = rs * (dh - jnp.mean(dh, axis=-1, keepdims=True) - h * jnp.mean(dh * h, axis=-1, keepdims=True))
            acc[q, :] = gr
            low = gr.astype(BF16)
            xg[q, :] = low
            return (sums[0] + fold(low.astype(F32)), sums[1] + fold(cot * h), sums[2] + fold(cot))

        sums = lax.fori_loop(0, rows // RT, step, (zero, zero, zero))
        put_out.start()
        va[0] = jnp.zeros((16, width), F32)
        for i, v in enumerate(sums):
            va[0, 2 + i : 3 + i, :] = jnp.sum(v, axis=0, keepdims=True)
        for b in range(blocks):
            r = slice(b * BLOCK, (b + 1) * BLOCK)
            for c in tiles:
                gt[c, r] = xg[r, c].T

    near, far_half = span(core * half, half), span((1 - core) * half, half)

    def unit(j):
        k, i = j // 2, j % 2
        return pout.at[k] if i == 0 else hid.at[target[k]]

    def part_rows(h, b, size):
        return span(core * half + h * (half // PARTS) + b * piece, size)

    def give(p, j):
        for h in range(PARTS):
            size = half // PARTS
            src = p.at[span((1 - core) * half + h * size, size)]
            send(src, r0.at[j, pl.ds(h * size, size)], s_h, hr.at[j, h], to_core)

    def unit_out(k, q):
        s = target[k]
        for c in htiles:
            pout[k, q, c] = mm(gt[q, :], hid[s, :, c]).astype(BF16)

    def out_far(k):
        unit_out(k, far_half)
        give(pout.at[k], 2 * k)

    def out_near(k):
        unit_out(k, near)

    def unit_pre(k, t):
        s = target[k]
        c = htiles[t]
        gp = (mm_t(xg[...], wout[s, c, :]) * slope[s, :, c].astype(F32)).astype(BF16)
        slope[s, :, c] = gp
        va[0, pl.ds(5 + s, 1), c] = jnp.sum(fold(gp.astype(F32)), axis=0, keepdims=True)

    def unit_in(k, q):
        s = target[k]
        for c in htiles:
            hid[s, q, c] = mm(xt[q, :], slope[s, :, c]).astype(BF16)

    def in_far(k):
        unit_in(k, far_half)
        give(hid.at[target[k]], 2 * k + 1)

    def in_near(k):
        unit_in(k, near)

    def add(a, b):
        return (a.astype(F32) + b.astype(F32)).astype(BF16)

    def u1(k, i, h):
        j = 2 * k + i
        p = unit(j)
        size = half // PARTS
        arrived(r0.at[j, pl.ds(h * size, size)], hr.at[j, h])
        for b, at, dev in ((1 - xx, 0, to_x), (2 + (1 - yy), 1, to_y)):
            q = part_rows(h, b, piece)
            p[q, :] = add(p[q, :], r0[j, span(h * size + b * piece, piece), :])
            send(p.at[q], rxy.at[j, h, at], s_t, tr.at[j, h], dev)

    def z_send(j, h, cond):
        k, i = j // 2, j % 2
        s = target[k]
        below = lax.div(n - 1 + m - s, n)
        last = 1 - lax.div(lax.rem(m - s - 1 + n, n) + (n - 1), n)
        slot = s + (n - s) * last
        send(rxy.at[j, h], rz.at[i, h, s], s_u, ur.at[i, h, s], up, cond & (below == 0))
        send(rxy.at[j, h], rz.at[i, h, slot], s_u, ur.at[i, h, slot], down, cond & (below == 1))

    def at_end(s):
        return ((s > m) & (m == 0)) | ((s < m) & (m == n - 1))

    def u2(k, i, h):
        j = 2 * k + i
        p = unit(j)
        size = half // PARTS
        arrived(rxy.at[j, h], tr.at[j, h])
        for b, at in ((xx, 0), (2 + yy, 1)):
            here = p[part_rows(h, b, piece), :].astype(F32) + r0[j, span(h * size + b * piece, piece), :].astype(F32)
            rxy[j, h, at] = (here + rxy[j, h, at].astype(F32)).astype(BF16)
        if k < n - 1:
            z_send(j, h, at_end(target[k]))

    def z_take(j, h, slot, cond):
        i = j % 2

        @pl.when(cond)
        def _():
            arrived(rz.at[i, h, slot], ur.at[i, h, slot])
            rxy[j, h] = add(rxy[j, h], rz[i, h, slot])

    def u3(k, i, h):
        j = 2 * k + i
        s = target[k]
        if k < n - 1:
            inner = jnp.logical_not(at_end(s))
            z_take(j, h, s, inner)
            z_send(j, h, inner)
        else:
            z_take(j, h, m, m > 0)
            z_take(j, h, n, m < n - 1)
            send(rxy.at[j, h, 0], rf.at[i, h, 0], s_fa, far.at[i, h], to_y)
            send(rxy.at[j, h, 1], rf.at[i, h, 1], s_fa, far.at[i, h], to_x)

    def fblock(i, h, b):
        return fin.at[i, part_rows(h, b, piece)]

    def f2(k, i, h):
        j = 2 * k + i
        arrived(rf.at[i, h], far.at[i, h])
        for b, at, dev in ((xx, 0, to_x), (2 + yy, 1, to_y)):
            block = fblock(i, h, b)
            block[...] = add(rxy[j, h, at], rf[i, h, at])
            send(block, block, s_fa, fbr.at[i, h], dev)

    def f3(k, i, h):
        arrived(rf.at[i, h], fbr.at[i, h])
        block = fin.at[i, part_rows(h, 0, half // PARTS)]
        send(block, block, s_fc, fcr.at[i], to_core)

    def f4(k, i):
        arrived(fin.at[i, far_half], fcr.at[i])
        if i == 0:
            for a in tiles:
                for c in htiles:
                    xg[c, a] = fin[0, a, c].T
            put_wout.start()
        else:
            put_win.start()

    def back_x(t):
        c = tiles[t]
        total = acc[:, c]
        for s in range(n):
            total = total + mm_t(slope[s], win[s, c, :])
        acc[:, c] = total

    def norm_one_back(t):
        if t == 0:
            put_out.wait()

        def step(i, sums):
            q = pl.ds(pl.multiple_of(i * RT, RT), RT)
            gn = acc[q, :]
            h = xhat[q, :]
            dh = gn * g1
            gs = rstd[q, :] * (dh - jnp.mean(dh, axis=-1, keepdims=True) - h * jnp.mean(dh * h, axis=-1, keepdims=True))
            acc[q, :] = gs
            tok[q, :] = gs.astype(BF16)
            return (sums[0] + fold(gn * h), sums[1] + fold(gn))

        steps = rows // RT
        start = (zero, zero) if t == 0 else (part[0:8, :], part[8:16, :])
        sums = lax.fori_loop(t * steps // 2, (t + 1) * steps // 2, step, start)
        for i, v in enumerate(sums):
            if t == 0:
                part[8 * i : 8 * i + 8, :] = v
            else:
                va[0, i : i + 1, :] = jnp.sum(v, axis=0, keepdims=True)

    def unmix_seq(b):
        r = slice(b * BLOCK, (b + 1) * BLOCK)
        k = kind[b]
        for c in tiles:
            by[0:BLOCK, c] = mm(seq[k, :, 0:BLOCK], tok[r, c]).astype(BF16)
            by[BLOCK : 2 * BLOCK, c] = mm(seq[k, :, BLOCK:], tok[r, c]).astype(BF16)

    def unmix_feat(b):
        r = slice(b * BLOCK, (b + 1) * BLOCK)
        for c in tiles:
            c2 = slice(c.start + width, c.stop + width)
            acc[r, c] = acc[r, c] + mm(by[0:BLOCK, :], feat[:, c]) + mm(by[BLOCK : 2 * BLOCK, :], feat[:, c2])

    def vec(t):
        if t > 0 and t < 4:
            arrived(vr.at[t - 1], vrr.at[t - 1])
            va[t] = va[t - 1] + vr[t - 1]
        if t < 3:
            send(va.at[t], vr.at[t], s_v, vrr.at[t], (to_core, to_x, to_y)[t])
        elif t == 3:
            vz[pl.ds(m, 1)] = va[pl.ds(3, 1)]
            for dev in others:
                send(va.at[3], vz.at[m], s_vz, once.at[1], dev)
        else:
            arrived(vz.at[pl.ds(0, n - 1)], once.at[1])
            total = vz[0]
            for s in range(1, n):
                total = total + vz[s]
            vec_out[...] = total
            vec_out[5:6, :] = vec_out[pl.ds(5 + m, 1), :]

    def unmix_out(b):
        unmix_feat(b)
        if b == blocks - 1:
            put_gt.start()

    ops = {
        "INIT": init, "DG": dg, "DF": df, "E1": e1, "E2": e2, "E3": e3, "E4": e4, "Ma": mix_feat, "Mb": mix_seq,
        "Mc": mix_norm, "A": fwd_a, "B": fwd_b, "N2": norm_two, "Oa": out_far, "Ob": out_near, "G": unit_pre,
        "Ia": in_far, "Ib": in_near, "U1": u1, "U2": u2, "U3": u3, "F2": f2, "F3": f3, "F4": f4, "X": back_x,
        "N1": norm_one_back, "Q": unmix_seq, "R": unmix_out, "V": vec,
    }
    for row in FORWARD + BACKWARD:
        for word in row.split():
            name, *numbers = word.split(".")
            ops[name](*map(int, numbers))
    for c in (put_gt, put_win, put_wout):
        c.wait()
    line = hid.at[0, pl.ds(0, 3 * PARTS * piece)]
    for s in range(n):
        pl.when((s <= m) & (m < n - 1))(functools.partial(all_sent, line, zs.at[0, s]))
        pl.when((s >= m) & (m > 0))(functools.partial(all_sent, line, zs.at[1, s]))
    for ref, sem in (
        (r0.at[pl.ds(0, n - 1)], s_xy), (hid.at[0, pl.ds(0, (n - 1) * PARTS * piece)], s_f), (win.at[pl.ds(0, n - 1)], s_c),
        (win, s_h), (r0.at[pl.ds(0, n)], s_t), (r0.at[pl.ds(0, n - 1)], s_u), (r0.at[pl.ds(0, 2)], s_fa),
        (r0.at[pl.ds(0, 2)], s_fc), (bias.at[pl.ds(0, n - 1)], s_b), (va.at[pl.ds(0, 3)], s_v), (vz.at[pl.ds(0, n - 1)], s_vz),
    ):
        all_sent(ref, sem)


def layer(n, kind, vectors, tokens, grad_out, feat, seq, w_in, w_out):
    rows, width = tokens.shape
    hidden = w_in.shape[1]
    half, piece, units = width // 2, width // (GROUP * PARTS), 2 * n
    any_spec = pl.BlockSpec(memory_space=pl.ANY)
    vmem = pl.BlockSpec(memory_space=pltpu.VMEM)
    dma = pltpu.SemaphoreType.DMA
    low = lambda *shape: pltpu.VMEM(shape, BF16)
    full = lambda *shape: pltpu.VMEM(shape, F32)
    return pl.pallas_call(
        functools.partial(layer_kernel, n),
        out_shape=(
            jax.ShapeDtypeStruct((rows, width), BF16),
            jax.ShapeDtypeStruct((rows, width), F32),
            jax.ShapeDtypeStruct((width, hidden), BF16),
            jax.ShapeDtypeStruct((hidden, width), BF16),
            jax.ShapeDtypeStruct((16, width), F32),
        ),
        in_specs=[pl.BlockSpec(memory_space=pltpu.SMEM)] + [vmem] * 6 + [any_spec] * 6,
        out_specs=[any_spec] * 4 + [vmem],
        scratch_shapes=[
            low(rows, width), low(*feat.shape), low(*seq.shape), low(n, width, hidden), low(n, hidden, width),
            low(n, rows, hidden), low(n, rows, hidden), full(rows, width), full(rows, width), low(rows, width),
            low(width, rows), low(width, rows), low(rows, width), full(rows, 1), full(n, 8, hidden), full(16, width),
            low(n, width, hidden), low(units, half, hidden), low(units, PARTS, 2, piece, hidden),
            low(2, PARTS, n + 1, 2, piece, hidden),
            low(2, PARTS, 2, piece, hidden), low(2, width, hidden), full(4, 16, width), full(3, 16, width), full(n, 16, width),
            dma((6,)), dma((11,)), dma((2, n)), dma((2, PARTS, n)), dma((PARTS, n)), dma((n - 1, PARTS)), dma((n - 1, PARTS)),
            dma((n - 1, PARTS)), dma((n - 1, PARTS)), dma((n - 1, 2)), dma((units, PARTS)), dma((units, PARTS)),
            dma((2, PARTS, n + 1)), dma((2, PARTS)), dma((2, PARTS)), dma((2,)), dma((3,)), dma((2,)),
        ],
        compiler_params=pltpu.CompilerParams(
            vmem_limit_bytes=VMEM_LIMIT, collective_id=0, has_side_effects=True
        ),
    )(kind, *vectors, tokens, grad_out, feat, seq, w_in, w_out)


def close_kernel(vec, out_in, gt_in, dwin_in, dwout_in, out, gt, dwin, dwout, *rest):
    vectors, (o, t, a, b, a_full, b_full, sems) = rest[:6], rest[6:]
    jobs = []
    for src, mid, wide, dst in (
        (dwin_in, a, a_full, dwin), (gt_in, t, t, gt), (dwout_in, b, b_full, dwout), (out_in, o, o, out)
    ):
        size = src.shape[0] // SPLIT
        for i in range(SPLIT):
            q = pl.ds(i * size, size)
            k = 2 * len(jobs)
            get = pltpu.make_async_copy(src.at[q], mid.at[q], sems.at[k])
            put = pltpu.make_async_copy(wide.at[q], dst.at[q], sems.at[k + 1])
            jobs.append((get, put, mid, wide, q))
    for job in jobs:
        job[0].start()
    for i, v in enumerate(vectors):
        v[...] = vec[i, :]
    for get, put, mid, wide, q in jobs:
        get.wait()
        if wide is not mid:
            wide[q, :] = mid[q, :].astype(F32)
        put.start()
    for job in jobs:
        job[1].wait()


def close(vec, out, gt, dwin, dwout):
    any_spec = pl.BlockSpec(memory_space=pl.ANY)
    vmem = pl.BlockSpec(memory_space=pltpu.VMEM)
    like = jax.ShapeDtypeStruct
    return pl.pallas_call(
        close_kernel,
        out_shape=[like(out.shape, BF16), like(gt.shape, F32), like(dwin.shape, F32), like(dwout.shape, F32)]
        + [like(vec.shape[1:], F32)] * 6,
        in_specs=[vmem] + [any_spec] * 4,
        out_specs=[any_spec] * 4 + [vmem] * 6,
        scratch_shapes=[
            pltpu.VMEM(out.shape, out.dtype), pltpu.VMEM(gt.shape, gt.dtype),
            pltpu.VMEM(dwin.shape, dwin.dtype), pltpu.VMEM(dwout.shape, dwout.dtype),
            pltpu.VMEM(dwin.shape, F32), pltpu.VMEM(dwout.shape, F32),
            pltpu.SemaphoreType.DMA((8 * SPLIT,)),
        ],
        compiler_params=pltpu.CompilerParams(vmem_limit_bytes=VMEM_LIMIT),
    )(vec, out, gt, dwin, dwout)


def local(
    tokens, block_kind, ln1_gain, ln1_bias, w_in, b_in, w_out, b_out, ln2_gain, ln2_bias, grad_out
):
    n_dp, n_mp = lax.axis_size("dp"), lax.axis_size("mp")
    feat = jnp.asarray(feature_table(tokens.shape[1]))
    seq = jnp.asarray(sequence_table())
    out, gt, dwin, dwout, vec = layer(
        n_mp, block_kind, (ln1_gain, ln1_bias, b_out, ln2_gain, ln2_bias, b_in), tokens, grad_out, feat, seq, w_in, w_out
    )
    shift = GROUP
    while shift < n_dp:
        turn = [(i, i // (2 * shift) * (2 * shift) + (i + shift) % (2 * shift)) for i in range(n_dp)]
        dwin, dwout = dwin.astype(F32), dwout.astype(F32)
        dwin, dwout, vec = (v + lax.ppermute(v, "dp", turn) for v in (dwin, dwout, vec))
        shift *= 2
    out, gt, dwin, dwout, gain1, bias1, bias_out, gain2, bias2, bias_in = close(vec, out, gt, dwin, dwout)
    return (out, gt, gain1, bias1, dwin, bias_in, dwout, bias_out, gain2, bias2)


def solution(mesh):
    in_specs = (
        P(("dp", "mp"), None),
        P(("dp", "mp")),
        P(),
        P(),
        P(None, "mp"),
        P("mp"),
        P("mp", None),
        P(),
        P(),
        P(),
        P(("dp", "mp"), None),
    )
    out_specs = (
        P(("dp", "mp"), None),
        P(("dp", "mp"), None),
        P(),
        P(),
        P(None, "mp"),
        P("mp"),
        P("mp", None),
        P(),
        P(),
        P(),
    )
    return jax.shard_map(local, mesh=mesh, in_specs=in_specs, out_specs=out_specs, check_vma=False)
```

```python
import functools
import math

import jax
import jax.numpy as jnp
import numpy as np
from jax import lax
from jax.experimental import pallas as pl
from jax.experimental.pallas import tpu as pltpu
from jax.sharding import PartitionSpec as P

BLOCK = 512
NT = 256
RT = 256
VMEM_LIMIT = 57 * 2**20
F32 = jnp.float32
BF16 = jnp.bfloat16
SQRT_2_PI = math.sqrt(2.0 / math.pi)


def sequence_table():
    ids = np.arange(BLOCK)
    out = []
    for variant in range(3):
        n = BLOCK // 2**variant
        place, owner = ids % n, ids // n
        same = owner[:, None] == owner[None, :]
        angle = (place[:, None] * place[None, :] % n) * (2.0 * math.pi / n)
        factor = 1.0 / math.sqrt(n)
        cos = np.where(same, np.cos(angle) * factor, 0.0)
        sin = np.where(same, np.sin(angle) * factor, 0.0)
        out.append(np.concatenate([cos, -sin], axis=1))
    return np.stack(out).astype(np.float32).astype(BF16)


def feature_table(n):
    ids = np.arange(n)
    angle = (ids[:, None] * ids[None, :] % n) * (2.0 * math.pi / n)
    factor = 1.0 / math.sqrt(n)
    return np.concatenate([np.cos(angle), np.sin(angle)], axis=1).astype(np.float32).__mul__(np.float32(factor)).astype(BF16)


def mm(a, b):
    return lax.dot_general(a, b, (((1,), (0,)), ((), ())), preferred_element_type=F32)


def mm_t(a, b):
    return lax.dot_general(a, b, (((1,), (1,)), ((), ())), preferred_element_type=F32)


def fold(v):
    return jnp.sum(v.reshape(v.shape[0] // 8, 8, v.shape[1]), axis=0)


def gelu_both(v):
    sq = v * v
    t = jnp.tanh(SQRT_2_PI * v * (1.0 + 0.044715 * sq))
    u = 0.5 * (1.0 + t)
    slope = u + (0.5 * SQRT_2_PI) * v * (1.0 - t * t) * (1.0 + (3 * 0.044715) * sq)
    return v * u, slope

MESH = pl.DeviceIdType.MESH
GROUP = 8

PARTS = 2

def pick(i, table):
    n = len(table)
    total = jnp.int32(0)
    for k, v in enumerate(table):
        total = total + v * (1 - lax.div(lax.rem(i - k + n, n) + (n - 1), n))
    return total


def layer_kernel(
    n, kind, g1_ref, s1_ref, bo_ref, g2_ref, s2_ref, bin_ref, tok_hbm, go_hbm, feat_hbm, seq_hbm, win_hbm, wout_hbm,
    tok, acc, dwin, dwout, vec_out,
    feat, seq, win, wout, hid, slope, xhat, xg, xt, gt, by, rstd, bias, part,
    pout, r0, rxy, rz, rf, fin, va, vr, vz,
    load_sem, sent, zs, zr, dr, xr, yr, xyr, fr, cr, hr, tr, ur, far, fbr, fcr, vrr, once,
):
    rows, width = tok.shape
    hidden = win.shape[2]
    blocks = rows // BLOCK
    weights, finals = (win, wout), (fin, dwin)
    d, m = lax.axis_index("dp"), lax.axis_index("mp")
    core, xx, yy = lax.rem(d, 2), lax.rem(lax.div(d, 2), 2), lax.rem(lax.div(d, 4), 2)
    to_core, to_x, to_y = (d + 1 - 2 * core, m), (d + 2 - 4 * xx, m), (d + 4 - 8 * yy, m)
    others = [(d, lax.rem(m + t, n)) for t in range(1, n)]
    up, down = (d, m + 1), (d, m - 1)
    foreign_order = [sorted((s for s in range(n) if s != mm), key=lambda s: (abs(s - mm), s)) for mm in range(n)]
    far_order = [sorted(range(n), key=lambda s: (-abs(s - mm), abs(2 * s - n + 1) * -1)) for mm in range(n)]
    foreign = [pick(m, [foreign_order[mm][k] for mm in range(n)]) for k in range(n - 1)]
    target = [pick(m, [far_order[mm][k] for mm in range(n)]) for k in range(n)]
    tiles = [slice(i * NT, (i + 1) * NT) for i in range(width // NT)]
    htiles = [slice(i * NT, (i + 1) * NT) for i in range(hidden // NT)]
    half = width // 2
    piece = half // (4 * PARTS)
    s_xy, s_f, s_c, s_h, s_t, s_u, s_fa, s_fc, s_b, s_v, s_vz = (sent.at[i] for i in range(11))

    def remote(src, dst, ssem, rsem, dev):
        return pltpu.make_async_remote_copy(
            src_ref=src, dst_ref=dst, send_sem=ssem, recv_sem=rsem, device_id=dev, device_id_type=MESH
        )

    def send(src, dst, ssem, rsem, dev, cond=None):
        copy = remote(src, dst, ssem, rsem, dev)
        if cond is None:
            copy.start()
        else:
            pl.when(cond)(copy.start)

    def all_sent(ref, sem):
        remote(ref, ref, sem, sem, to_core).wait_send()

    def arrived(dst, rsem):
        remote(dst, dst, rsem, rsem, to_core).wait_recv()

    barrier = pltpu.get_barrier_semaphore()
    partners = [to_core, to_x, to_y] + others
    for dev in partners:
        pl.semaphore_signal(barrier, inc=1, device_id=dev, device_id_type=MESH)
    loads = [
        pltpu.make_async_copy(a, b, load_sem.at[i])
        for i, (a, b) in enumerate(
            [(tok_hbm, tok), (feat_hbm, feat), (seq_hbm, seq), (win_hbm, win.at[m]), (wout_hbm, wout.at[m]), (go_hbm, by)]
        )
    ]
    for c in loads[:5]:
        c.start()
    g1, s1, bo, g2, s2 = (
        r[...].astype(F32).reshape(1, width) for r in (g1_ref, s1_ref, bo_ref, g2_ref, s2_ref)
    )
    bias[pl.ds(m, 1)] = jnp.broadcast_to(bin_ref[...].astype(F32).reshape(1, 1, hidden), (1, 8, hidden))
    pl.semaphore_wait(barrier, len(partners))

    def span(start, size):
        return pl.ds(pl.multiple_of(start, 16), size)

    mine, by_x, by_y, diag = 2 * yy + xx, 2 * yy + (1 - xx), 2 * (1 - yy) + xx, 2 * (1 - yy) + (1 - xx)

    def rows_of(w, h, q):
        size = w.shape[0] // (GROUP * PARTS)
        return span(((core * PARTS + h) * 4 + q) * size, size)

    def wblock(i, s, h, q):
        return weights[i].at[s, rows_of(weights[i].at[0], h, q)]

    def wpart(i, s, h, c):
        size = weights[i].shape[1] // (2 * PARTS)
        return weights[i].at[s, span((c * PARTS + h) * size, size)]

    def along(s, src, dst, rsem):
        send(src, dst, zs.at[0, s], rsem, up, (s <= m) & (m < n - 1))
        send(src, dst, zs.at[1, s], rsem, down, (s >= m) & (m > 0))

    def init():
        for i, w in enumerate((win_hbm, wout_hbm)):
            for h in range(PARTS):
                along(m, w.at[rows_of(w, h, mine)], wblock(i, m, h, mine), zr.at[i, h, m])
            if i == 0:
                for dev in others:
                    send(bias.at[m], bias.at[m], s_b, once.at[0], dev)

    def dg(i, h):
        w = (win_hbm, wout_hbm)[i]
        along(m, w.at[rows_of(w, h, diag)], wblock(i, m, h, diag), dr.at[h, m])

    def df(k, i, h):
        s = foreign[k]
        block = wblock(i, s, h, diag)

        @pl.when(((s < m) & (m < n - 1)) | ((s > m) & (m > 0)))
        def _():
            arrived(block, dr.at[h, s])

        along(s, block, block, dr.at[h, s])

    def e1(k, i, h):
        s = foreign[k]
        block = wblock(i, s, h, mine)
        arrived(block, zr.at[i, h, s])
        send(block, block, s_xy, (xr, xyr)[i].at[k, h], to_x)
        send(block, block, s_xy, (yr, xyr)[i].at[k, h], to_y)
        along(s, block, block, zr.at[i, h, s])

    def e2(k, i, h):
        s = foreign[k]
        if i == 1:
            return
        if h % 2 == 0:
            block = wblock(i, s, h, by_x)
            arrived(block, xr.at[k, h])
            send(block, block, s_f, fr.at[k, h], to_y)
        else:
            block = wblock(i, s, h, by_y)
            arrived(block, yr.at[k, h])
            send(block, block, s_f, fr.at[k, h], to_x)

    def e3(k, i, h):
        s = foreign[k]
        if i == 0:
            if h % 2 == 0:
                arrived(wblock(i, s, h, by_y), yr.at[k, h])
            else:
                arrived(wblock(i, s, h, by_x), xr.at[k, h])
            arrived(wblock(i, s, h, diag), fr.at[k, h])
        else:
            arrived(wout.at[s, pl.ds(0, 2 * piece)], xyr.at[k, h])
            at_edge = ((s < m) & (m == n - 1)) | ((s > m) & (m == 0))

            @pl.when(at_edge)
            def _():
                arrived(wblock(i, s, h, diag), dr.at[h, s])

        block = wpart(i, s, h, core)
        send(block, block, s_c, cr.at[k, i], to_core)

    def e4(k, i):
        s = foreign[k]
        arrived(weights[i].at[s, span((1 - core) * half, half)], cr.at[k, i])
        if i == 0 and k == 0:
            arrived(bias.at[pl.ds(0, n - 1)], once.at[0])

    def mix_feat(b):
        if b == 0:
            loads[0].wait()
            loads[1].wait()
        r = slice(b * BLOCK, (b + 1) * BLOCK)
        for c in tiles:
            by[0:BLOCK, c] = mm(tok[r, :], feat[:, c]).astype(BF16)
            c2 = slice(c.start + width, c.stop + width)
            by[BLOCK : 2 * BLOCK, c] = mm(tok[r, :], feat[:, c2]).astype(BF16)

    def mix_seq(b):
        if b == 0:
            loads[2].wait()
        r = slice(b * BLOCK, (b + 1) * BLOCK)
        k = kind[b]
        for c in tiles:
            xhat[r, c] = tok[r, c].astype(F32) + mm(seq[k], by[:, c])

    def mix_norm(b):
        r = slice(b * BLOCK, (b + 1) * BLOCK)

        def norm_one(i, _):
            q = pl.ds(pl.multiple_of(b * BLOCK + i * RT, RT), RT)
            v = xhat[q, :]
            centre = v - jnp.mean(v, axis=-1, keepdims=True)
            rs = lax.rsqrt(jnp.mean(centre * centre, axis=-1, keepdims=True) + 1e-5)
            h = centre * rs
            xhat[q, :] = h
            rstd[q, :] = rs
            xg[q, :] = (h * g1 + s1).astype(BF16)
            return 0

        lax.fori_loop(0, BLOCK // RT, norm_one, 0)
        for c in tiles:
            xt[c, r] = xg[r, c].T
        if b == blocks - 1:
            loads[5].start()

    def fwd_a(f, t):
        if f == 0 and t == 0:
            loads[3].wait()
        s = m if f == 0 else foreign[f - 1]
        c = htiles[t]
        pre = mm(xg[...], win[s, :, c]) + bias[s, 0:1, c]
        a, dv = gelu_both(pre)
        hid[s, :, c] = a.astype(BF16)
        slope[s, :, c] = dv.astype(BF16)

    def fwd_b(f, t):
        if f == 0 and t == 0:
            loads[4].wait()
        s = m if f == 0 else foreign[f - 1]
        c = tiles[t]
        term = mm(hid[s], wout[s, :, c])
        acc[:, c] = term if f == 0 else acc[:, c] + term

    zero = jnp.zeros((8, width), F32)
    def norm_two():
        loads[5].wait()

        def step(i, sums):
            q = pl.ds(pl.multiple_of(i * RT, RT), RT)
            v = xhat[q, :] * g1 + s1 + (acc[q, :] + bo)
            centre = v - jnp.mean(v, axis=-1, keepdims=True)
            rs = lax.rsqrt(jnp.mean(centre * centre, axis=-1, keepdims=True) + 1e-5)
            h = centre * rs
            tok[q, :] = (h * g2 + s2).astype(BF16)
            cot = by[q, :].astype(F32)
            dh = cot * g2
            gr = rs * (dh - jnp.mean(dh, axis=-1, keepdims=True) - h * jnp.mean(dh * h, axis=-1, keepdims=True))
            acc[q, :] = gr
            low = gr.astype(BF16)
            xg[q, :] = low
            return (sums[0] + fold(low.astype(F32)), sums[1] + fold(cot * h), sums[2] + fold(cot))

        sums = lax.fori_loop(0, rows // RT, step, (zero, zero, zero))
        va[0] = jnp.zeros((16, width), F32)
        for i, v in enumerate(sums):
            va[0, 2 + i : 3 + i, :] = jnp.sum(v, axis=0, keepdims=True)
        for b in range(blocks):
            r = slice(b * BLOCK, (b + 1) * BLOCK)
            for c in tiles:
                gt[c, r] = xg[r, c].T

    near, far_half = span(core * half, half), span((1 - core) * half, half)

    def unit(j):
        k, i = j // 2, j % 2
        return pout.at[k] if i == 0 else hid.at[target[k]]

    def part_rows(h, b, size):
        return span(core * half + h * (half // PARTS) + b * piece, size)

    def give(p, j):
        for h in range(PARTS):
            size = half // PARTS
            src = p.at[span((1 - core) * half + h * size, size)]
            send(src, r0.at[j, pl.ds(h * size, size)], s_h, hr.at[j, h], to_core)

    def unit_out(k, q):
        s = target[k]
        for c in htiles:
            pout[k, q, c] = mm(gt[q, :], hid[s, :, c]).astype(BF16)

    def out_far(k):
        unit_out(k, far_half)
        give(pout.at[k], 2 * k)

    def out_near(k):
        unit_out(k, near)

    def unit_pre(k, t):
        s = target[k]
        c = htiles[t]
        gp = (mm_t(xg[...], wout[s, c, :]) * slope[s, :, c].astype(F32)).astype(BF16)
        slope[s, :, c] = gp
        va[0, pl.ds(5 + s, 1), c] = jnp.sum(fold(gp.astype(F32)), axis=0, keepdims=True)

    def unit_in(k, q):
        s = target[k]
        for c in htiles:
            hid[s, q, c] = mm(xt[q, :], slope[s, :, c]).astype(BF16)

    def in_far(k):
        unit_in(k, far_half)
        give(hid.at[target[k]], 2 * k + 1)

    def in_near(k):
        unit_in(k, near)

    def add(a, b):
        return (a.astype(F32) + b.astype(F32)).astype(BF16)

    def u1(k, i, h):
        j = 2 * k + i
        p = unit(j)
        size = half // PARTS
        arrived(r0.at[j, pl.ds(h * size, size)], hr.at[j, h])
        for b, at, dev in ((1 - xx, 0, to_x), (2 + (1 - yy), 1, to_y)):
            q = part_rows(h, b, piece)
            p[q, :] = add(p[q, :], r0[j, span(h * size + b * piece, piece), :])
            send(p.at[q], rxy.at[j, h, at], s_t, tr.at[j, h], dev)

    def z_send(j, h, cond):
        k, i = j // 2, j % 2
        s = target[k]
        below = lax.div(n - 1 + m - s, n)
        last = 1 - lax.div(lax.rem(m - s - 1 + n, n) + (n - 1), n)
        slot = s + (n - s) * last
        send(rxy.at[j, h], rz.at[i, h, s], s_u, ur.at[i, h, s], up, cond & (below == 0))
        send(rxy.at[j, h], rz.at[i, h, slot], s_u, ur.at[i, h, slot], down, cond & (below == 1))

    def at_end(s):
        return ((s > m) & (m == 0)) | ((s < m) & (m == n - 1))

    def u2(k, i, h):
        j = 2 * k + i
        p = unit(j)
        size = half // PARTS
        arrived(rxy.at[j, h], tr.at[j, h])
        for b, at in ((xx, 0), (2 + yy, 1)):
            here = p[part_rows(h, b, piece), :].astype(F32) + r0[j, span(h * size + b * piece, piece), :].astype(F32)
            rxy[j, h, at] = (here + rxy[j, h, at].astype(F32)).astype(BF16)
        if k < n - 1:
            z_send(j, h, at_end(target[k]))

    def z_take(j, h, slot, cond):
        i = j % 2

        @pl.when(cond)
        def _():
            arrived(rz.at[i, h, slot], ur.at[i, h, slot])
            rxy[j, h] = add(rxy[j, h], rz[i, h, slot])

    def u3(k, i, h):
        j = 2 * k + i
        s = target[k]
        if k < n - 1:
            inner = jnp.logical_not(at_end(s))
            z_take(j, h, s, inner)
            z_send(j, h, inner)
        else:
            z_take(j, h, m, m > 0)
            z_take(j, h, n, m < n - 1)
            send(rxy.at[j, h, 0], rf.at[i, h, 0], s_fa, far.at[i, h], to_y)
            send(rxy.at[j, h, 1], rf.at[i, h, 1], s_fa, far.at[i, h], to_x)

    def fblock(i, h, b):
        return finals[i].at[part_rows(h, b, piece)]

    def f2(k, i, h):
        j = 2 * k + i
        arrived(rf.at[i, h], far.at[i, h])
        for b, at, dev in ((xx, 0, to_x), (2 + yy, 1, to_y)):
            block = fblock(i, h, b)
            block[...] = add(rxy[j, h, at], rf[i, h, at])
            send(block, block, s_fa, fbr.at[i, h], dev)

    def f3(k, i, h):
        arrived(rf.at[i, h], fbr.at[i, h])
        block = finals[i].at[part_rows(h, 0, half // PARTS)]
        send(block, block, s_fc, fcr.at[i], to_core)

    def f4(k, i):
        arrived(finals[i].at[far_half], fcr.at[i])
        if i == 0:
            for a in tiles:
                for c in htiles:
                    dwout[c, a] = fin[a, c].T

    def back_x(t):
        c = tiles[t]
        total = acc[:, c]
        for s in range(n):
            total = total + mm_t(slope[s], win[s, c, :])
        acc[:, c] = total

    def norm_one_back(t):
        def step(i, sums):
            q = pl.ds(pl.multiple_of(i * RT, RT), RT)
            gn = acc[q, :]
            h = xhat[q, :]
            dh = gn * g1
            gs = rstd[q, :] * (dh - jnp.mean(dh, axis=-1, keepdims=True) - h * jnp.mean(dh * h, axis=-1, keepdims=True))
            acc[q, :] = gs
            xg[q, :] = gs.astype(BF16)
            return (sums[0] + fold(gn * h), sums[1] + fold(gn))

        steps = rows // RT
        start = (zero, zero) if t == 0 else (part[0:8, :], part[8:16, :])
        sums = lax.fori_loop(t * steps // 2, (t + 1) * steps // 2, step, start)
        for i, v in enumerate(sums):
            if t == 0:
                part[8 * i : 8 * i + 8, :] = v
            else:
                va[0, i : i + 1, :] = jnp.sum(v, axis=0, keepdims=True)

    def unmix_seq(b):
        r = slice(b * BLOCK, (b + 1) * BLOCK)
        k = kind[b]
        for c in tiles:
            by[0:BLOCK, c] = mm(seq[k, :, 0:BLOCK], xg[r, c]).astype(BF16)
            by[BLOCK : 2 * BLOCK, c] = mm(seq[k, :, BLOCK:], xg[r, c]).astype(BF16)

    def unmix_feat(b):
        r = slice(b * BLOCK, (b + 1) * BLOCK)
        for c in tiles:
            c2 = slice(c.start + width, c.stop + width)
            acc[r, c] = acc[r, c] + mm(by[0:BLOCK, :], feat[:, c]) + mm(by[BLOCK : 2 * BLOCK, :], feat[:, c2])

    def vec(t):
        if t > 0 and t < 4:
            arrived(vr.at[t - 1], vrr.at[t - 1])
            va[t] = va[t - 1] + vr[t - 1]
        if t < 3:
            send(va.at[t], vr.at[t], s_v, vrr.at[t], (to_core, to_x, to_y)[t])
        elif t == 3:
            vz[pl.ds(m, 1)] = va[pl.ds(3, 1)]
            for dev in others:
                send(va.at[3], vz.at[m], s_vz, once.at[1], dev)
        else:
            arrived(vz.at[pl.ds(0, n - 1)], once.at[1])
            total = vz[0]
            for s in range(1, n):
                total = total + vz[s]
            vec_out[...] = total
            vec_out[5:6, :] = vec_out[pl.ds(5 + m, 1), :]

    init()
    mix_feat(0)
    mix_seq(0)
    e1(0, 0, 0)
    mix_norm(0)
    e1(0, 0, 1)
    mix_feat(1)
    e1(0, 1, 0)
    e2(0, 0, 0)
    e1(1, 0, 1)
    dg(1, 0)
    mix_seq(1)
    e2(0, 0, 1)
    mix_norm(1)
    e1(1, 0, 0)
    dg(1, 1)
    fwd_a(0, 0)
    e1(0, 1, 1)
    fwd_a(0, 1)
    fwd_a(0, 2)
    e3(0, 0, 0)
    fwd_b(0, 0)
    e1(2, 0, 1)
    e2(1, 0, 1)
    e2(0, 1, 0)
    fwd_b(0, 1)
    e3(0, 0, 1)
    fwd_b(0, 2)
    df(0, 1, 0)
    e2(1, 0, 0)
    e1(2, 0, 0)
    e3(0, 1, 0)
    e4(0, 0)
    fwd_a(1, 0)
    e1(1, 1, 1)
    fwd_a(1, 1)
    df(0, 1, 1)
    e2(1, 1, 1)
    e2(0, 1, 1)
    e3(0, 1, 1)
    fwd_a(1, 2)
    e1(1, 1, 0)
    e2(2, 0, 1)
    e4(0, 1)
    fwd_b(1, 0)
    e3(1, 0, 0)
    df(1, 1, 1)
    e3(1, 0, 1)
    fwd_b(1, 1)
    fwd_b(1, 2)
    e2(2, 0, 0)
    e1(2, 1, 1)
    e4(1, 0)
    fwd_a(2, 0)
    df(1, 1, 0)
    fwd_a(2, 1)
    e2(1, 1, 0)
    e3(1, 1, 1)
    fwd_a(2, 2)
    e3(1, 1, 0)
    e1(2, 1, 0)
    e2(2, 1, 0)
    df(2, 1, 1)
    df(2, 1, 0)
    e3(2, 0, 1)
    e3(2, 0, 0)
    e2(2, 1, 1)
    e4(1, 1)
    fwd_b(2, 0)
    fwd_b(2, 1)
    fwd_b(2, 2)
    e3(2, 1, 1)
    e4(2, 0)
    fwd_a(3, 0)
    e3(2, 1, 0)
    fwd_a(3, 1)
    fwd_a(3, 2)
    e4(2, 1)
    fwd_b(3, 0)
    fwd_b(3, 1)
    fwd_b(3, 2)
    norm_two()
    out_far(0)
    out_far(1)
    out_near(0)
    u1(0, 0, 1)
    out_far(2)
    u1(0, 0, 0)
    unit_pre(3, 0)
    out_near(1)
    unit_pre(0, 0)
    u2(0, 0, 1)
    u1(1, 0, 0)
    out_far(3)
    u1(1, 0, 1)
    out_near(2)
    u2(0, 0, 0)
    unit_pre(0, 1)
    u1(2, 0, 0)
    out_near(3)
    unit_pre(0, 2)
    u1(3, 0, 1)
    u3(0, 0, 1)
    u2(1, 0, 0)
    in_far(0)
    u1(2, 0, 1)
    u2(2, 0, 0)
    in_near(0)
    u1(0, 1, 0)
    u3(0, 0, 0)
    unit_pre(1, 0)
    unit_pre(1, 1)
    u1(0, 1, 1)
    u1(3, 0, 0)
    unit_pre(1, 2)
    in_far(1)
    u3(2, 0, 0)
    u2(1, 0, 1)
    u3(1, 0, 1)
    in_near(1)
    unit_pre(2, 0)
    u3(1, 0, 0)
    u1(1, 1, 1)
    unit_pre(2, 1)
    unit_pre(2, 2)
    u1(1, 1, 0)
    in_far(2)
    u2(0, 1, 0)
    in_near(2)
    u2(2, 0, 1)
    u1(2, 1, 0)
    u3(2, 0, 1)
    unit_pre(3, 1)
    unit_pre(3, 2)
    u1(2, 1, 1)
    in_far(3)
    u2(0, 1, 1)
    in_near(3)
    u2(1, 1, 0)
    u1(3, 1, 0)
    u3(0, 1, 0)
    u2(1, 1, 1)
    u1(3, 1, 1)
    back_x(0)
    u2(3, 0, 0)
    u3(3, 0, 0)
    back_x(1)
    u3(0, 1, 1)
    u3(1, 1, 0)
    u2(3, 0, 1)
    u3(3, 0, 1)
    back_x(2)
    u2(2, 1, 0)
    u3(2, 1, 0)
    f2(3, 0, 0)
    norm_one_back(0)
    norm_one_back(1)
    vec(0)
    u3(1, 1, 1)
    u2(2, 1, 1)
    u3(2, 1, 1)
    vec(1)
    f2(3, 0, 1)
    f3(3, 0, 0)
    u2(3, 1, 1)
    unmix_seq(0)
    u2(3, 1, 0)
    vec(2)
    u3(3, 1, 0)
    unmix_feat(0)
    u3(3, 1, 1)
    vec(3)
    f3(3, 0, 1)
    f2(3, 1, 0)
    unmix_seq(1)
    f2(3, 1, 1)
    unmix_feat(1)
    f3(3, 1, 0)
    f4(3, 0)
    f3(3, 1, 1)
    vec(4)
    f4(3, 1)
    line = hid.at[0, pl.ds(0, 3 * PARTS * piece)]
    for s in range(n):
        pl.when((s <= m) & (m < n - 1))(functools.partial(all_sent, line, zs.at[0, s]))
        pl.when((s >= m) & (m > 0))(functools.partial(all_sent, line, zs.at[1, s]))
    for ref, sem in (
        (r0.at[pl.ds(0, n - 1)], s_xy), (hid.at[0, pl.ds(0, (n - 1) * PARTS * piece)], s_f), (win.at[pl.ds(0, n - 1)], s_c),
        (win, s_h), (r0.at[pl.ds(0, n)], s_t), (r0.at[pl.ds(0, n - 1)], s_u), (r0.at[pl.ds(0, 2)], s_fa),
        (r0.at[pl.ds(0, 2)], s_fc), (bias.at[pl.ds(0, n - 1)], s_b), (va.at[pl.ds(0, 3)], s_v), (vz.at[pl.ds(0, n - 1)], s_vz),
    ):
        all_sent(ref, sem)


def layer(n, kind, vectors, tokens, grad_out, feat, seq, w_in, w_out):
    rows, width = tokens.shape
    hidden = w_in.shape[1]
    half, piece, units = width // 2, width // (GROUP * PARTS), 2 * n
    any_spec = pl.BlockSpec(memory_space=pl.ANY)
    vmem = pl.BlockSpec(memory_space=pltpu.VMEM)
    dma = pltpu.SemaphoreType.DMA
    low = lambda *shape: pltpu.VMEM(shape, BF16)
    full = lambda *shape: pltpu.VMEM(shape, F32)
    return pl.pallas_call(
        functools.partial(layer_kernel, n),
        out_shape=(
            low(rows, width),
            full(rows, width),
            low(width, hidden),
            low(hidden, width),
            full(16, width),
        ),
        in_specs=[pl.BlockSpec(memory_space=pltpu.SMEM)] + [vmem] * 6 + [any_spec] * 6,
        out_specs=[vmem] * 5,
        scratch_shapes=[
            low(*feat.shape), low(*seq.shape), low(n, width, hidden), low(n, hidden, width),
            low(n, rows, hidden), low(n, rows, hidden), full(rows, width), low(rows, width),
            low(width, rows), low(width, rows), low(rows, width), full(rows, 1), full(n, 8, hidden), full(16, width),
            low(n, width, hidden), low(units, half, hidden), low(units, PARTS, 2, piece, hidden),
            low(2, PARTS, n + 1, 2, piece, hidden),
            low(2, PARTS, 2, piece, hidden), low(width, hidden), full(4, 16, width), full(3, 16, width), full(n, 16, width),
            dma((6,)), dma((11,)), dma((2, n)), dma((2, PARTS, n)), dma((PARTS, n)), dma((n - 1, PARTS)), dma((n - 1, PARTS)),
            dma((n - 1, PARTS)), dma((n - 1, PARTS)), dma((n - 1, 2)), dma((units, PARTS)), dma((units, PARTS)),
            dma((2, PARTS, n + 1)), dma((2, PARTS)), dma((2, PARTS)), dma((2,)), dma((3,)), dma((2,)),
        ],
        compiler_params=pltpu.CompilerParams(
            vmem_limit_bytes=VMEM_LIMIT, collective_id=0, has_side_effects=True
        ),
    )(kind, *vectors, tokens, grad_out, feat, seq, w_in, w_out)


def close_kernel(vec, out_in, gt_in, dwin_in, dwout_in, out, gt, dwin, dwout, *rest):
    vectors, (a, b, sems) = rest[:6], rest[6:]
    puts = [pltpu.make_async_copy(x, y, sems.at[i]) for i, (x, y) in enumerate(((gt_in, gt), (out_in, out), (a, dwin), (b, dwout)))]
    puts[0].start()
    puts[1].start()
    for p, x, y in ((puts[2], dwin_in, a), (puts[3], dwout_in, b)):
        y[...] = x[...].astype(F32)
        p.start()
    for i, v in enumerate(vectors):
        v[...] = vec[i, :]
    for p in puts:
        p.wait()


def close(vec, *arrays):
    vec, out, gt, dwin, dwout = (pltpu.with_memory_space_constraint(v, pltpu.VMEM) for v in (vec, *arrays))
    any_spec = pl.BlockSpec(memory_space=pl.ANY)
    vmem = pl.BlockSpec(memory_space=pltpu.VMEM)
    like = jax.ShapeDtypeStruct
    return pl.pallas_call(
        close_kernel,
        out_shape=[like(out.shape, BF16), like(gt.shape, F32), like(dwin.shape, F32), like(dwout.shape, F32)]
        + [like(vec.shape[1:], F32)] * 6,
        in_specs=[vmem] * 5,
        out_specs=[any_spec] * 4 + [vmem] * 6,
        scratch_shapes=[
            pltpu.VMEM(dwin.shape, F32), pltpu.VMEM(dwout.shape, F32), pltpu.SemaphoreType.DMA((4,)),
        ],
        compiler_params=pltpu.CompilerParams(vmem_limit_bytes=40 * 2**20),
    )(vec, out, gt, dwin, dwout)


def local(
    tokens, block_kind, ln1_gain, ln1_bias, w_in, b_in, w_out, b_out, ln2_gain, ln2_bias, grad_out
):
    n_dp, n_mp = lax.axis_size("dp"), lax.axis_size("mp")
    feat = jnp.asarray(feature_table(tokens.shape[1]))
    seq = jnp.asarray(sequence_table())
    out, gt, dwin, dwout, vec = layer(
        n_mp, block_kind, (ln1_gain, ln1_bias, b_out, ln2_gain, ln2_bias, b_in), tokens, grad_out, feat, seq, w_in, w_out
    )
    shift = GROUP
    while shift < n_dp:
        turn = [(i, i // (2 * shift) * (2 * shift) + (i + shift) % (2 * shift)) for i in range(n_dp)]
        dwin, dwout = dwin.astype(F32), dwout.astype(F32)
        dwin, dwout, vec = (v + lax.ppermute(v, "dp", turn) for v in (dwin, dwout, vec))
        shift *= 2
    out, gt, dwin, dwout, gain1, bias1, bias_out, gain2, bias2, bias_in = close(vec, out, gt, dwin, dwout)
    return (out, gt, gain1, bias1, dwin, bias_in, dwout, bias_out, gain2, bias2)


def solution(mesh):
    in_specs = (
        P(("dp", "mp"), None),
        P(("dp", "mp")),
        P(),
        P(),
        P(None, "mp"),
        P("mp"),
        P("mp", None),
        P(),
        P(),
        P(),
        P(("dp", "mp"), None),
    )
    out_specs = (
        P(("dp", "mp"), None),
        P(("dp", "mp"), None),
        P(),
        P(),
        P(None, "mp"),
        P("mp"),
        P("mp", None),
        P(),
        P(),
        P(),
    )
    return jax.shard_map(local, mesh=mesh, in_specs=in_specs, out_specs=out_specs, check_vma=False)
```

```python
import functools
import math

import jax
import jax.numpy as jnp
import numpy as np
from jax import lax
from jax.experimental import pallas as pl
from jax.experimental.pallas import tpu as pltpu
from jax.sharding import PartitionSpec as P

BLOCK = 512
NT = 256
RT = 256
VMEM_LIMIT = 57 * 2**20
F32 = jnp.float32
BF16 = jnp.bfloat16
SQRT_2_PI = math.sqrt(2.0 / math.pi)


def sequence_table():
    ids = np.arange(BLOCK)
    out = []
    for variant in range(3):
        n = BLOCK // 2**variant
        place, owner = ids % n, ids // n
        same = owner[:, None] == owner[None, :]
        angle = (place[:, None] * place[None, :] % n) * (2.0 * math.pi / n)
        factor = 1.0 / math.sqrt(n)
        cos = np.where(same, np.cos(angle) * factor, 0.0)
        sin = np.where(same, np.sin(angle) * factor, 0.0)
        out.append(np.concatenate([cos, -sin], axis=1))
    return np.stack(out).astype(np.float32).astype(BF16)


def feature_table(n):
    ids = np.arange(n)
    angle = (ids[:, None] * ids[None, :] % n) * (2.0 * math.pi / n)
    factor = 1.0 / math.sqrt(n)
    return np.concatenate([np.cos(angle), np.sin(angle)], axis=1).astype(np.float32).__mul__(np.float32(factor)).astype(BF16)


def mm(a, b):
    return lax.dot_general(a, b, (((1,), (0,)), ((), ())), preferred_element_type=F32)


def mm_t(a, b):
    return lax.dot_general(a, b, (((1,), (1,)), ((), ())), preferred_element_type=F32)


def fold(v):
    return jnp.sum(v.reshape(v.shape[0] // 8, 8, v.shape[1]), axis=0)


def gelu_both(v):
    sq = v * v
    t = jnp.tanh(SQRT_2_PI * v * (1.0 + 0.044715 * sq))
    u = 0.5 * (1.0 + t)
    slope = u + (0.5 * SQRT_2_PI) * v * (1.0 - t * t) * (1.0 + (3 * 0.044715) * sq)
    return v * u, slope

MESH = pl.DeviceIdType.MESH
GROUP = 8

PARTS = 2

def pick(i, table):
    n = len(table)
    total = jnp.int32(0)
    for k, v in enumerate(table):
        total = total + v * (1 - lax.div(lax.rem(i - k + n, n) + (n - 1), n))
    return total


def layer_kernel(
    n, kind, g1_ref, s1_ref, bo_ref, g2_ref, s2_ref, bin_ref, tok_hbm, go_hbm, feat_hbm, seq_hbm, win_hbm, wout_hbm,
    tok, acc, dwin, dwout, vec_out,
    feat, seq, win, wout, hid, slope, xhat, xg, xt, gt, by, rstd, bias, part,
    pout, r0, rxy, rz, rf, fin, va, vr, vz,
    load_sem, sent, zs, zr, dr, xr, yr, xyr, fr, cr, hr, tr, ur, far, fbr, fcr, vrr, once,
):
    rows, width = tok.shape
    hidden = win.shape[2]
    blocks = rows // BLOCK
    weights, finals = (win, wout), (fin, dwin)
    d, m = lax.axis_index("dp"), lax.axis_index("mp")
    core, xx, yy = lax.rem(d, 2), lax.rem(lax.div(d, 2), 2), lax.rem(lax.div(d, 4), 2)
    to_core, to_x, to_y = (d + 1 - 2 * core, m), (d + 2 - 4 * xx, m), (d + 4 - 8 * yy, m)
    others = [(d, lax.rem(m + t, n)) for t in range(1, n)]
    up, down = (d, m + 1), (d, m - 1)
    held = [[mm] + sorted((s for s in range(n) if s != mm), key=lambda s: (abs(s - mm), s)) for mm in range(n)]
    shard = [pick(m, [held[mm][f] for mm in range(n)]) for f in range(n)]

    ends_first = [sorted(range(n), key=lambda s: (-abs(s - mm), -abs(2 * s - n + 1))) for mm in range(n)]
    slot = [pick(m, [held[mm].index(ends_first[mm][k]) for mm in range(n)]) for k in range(n)]
    target = [pick(m, [ends_first[mm][k] for mm in range(n)]) for k in range(n)]

    def slot_at(step, f):
        return pick(m, [held[mm + step].index(held[mm][f]) if 0 <= mm + step < n else 0 for mm in range(n)])

    slot_up, slot_down = ([slot_at(step, f) for f in range(n)] for step in (1, -1))
    tiles = [slice(i * NT, (i + 1) * NT) for i in range(width // NT)]
    htiles = [slice(i * NT, (i + 1) * NT) for i in range(hidden // NT)]
    half = width // 2
    piece = half // (4 * PARTS)
    s_xy, s_f, s_c, s_h, s_t, s_u, s_fa, s_fc, s_b, s_v, s_vz = (sent.at[i] for i in range(11))

    def remote(src, dst, ssem, rsem, dev):
        return pltpu.make_async_remote_copy(
            src_ref=src, dst_ref=dst, send_sem=ssem, recv_sem=rsem, device_id=dev, device_id_type=MESH
        )

    def send(src, dst, ssem, rsem, dev, cond=None):
        copy = remote(src, dst, ssem, rsem, dev)
        if cond is None:
            copy.start()
        else:
            pl.when(cond)(copy.start)

    def all_sent(ref, sem):
        remote(ref, ref, sem, sem, to_core).wait_send()

    def arrived(dst, rsem):
        remote(dst, dst, rsem, rsem, to_core).wait_recv()

    barrier = pltpu.get_barrier_semaphore()
    partners = [to_core, to_x, to_y] + others
    for dev in partners:
        pl.semaphore_signal(barrier, inc=1, device_id=dev, device_id_type=MESH)
    loads = [
        pltpu.make_async_copy(a, b, load_sem.at[i])
        for i, (a, b) in enumerate(
            [(tok_hbm, tok), (feat_hbm, feat), (seq_hbm, seq), (win_hbm, win.at[0]), (wout_hbm, wout.at[0]), (go_hbm, by)]
        )
    ]
    for c in loads[:5]:
        c.start()
    g1, s1, bo, g2, s2 = (
        r[...].astype(F32).reshape(1, width) for r in (g1_ref, s1_ref, bo_ref, g2_ref, s2_ref)
    )
    bias[0:1] = jnp.broadcast_to(bin_ref[...].astype(F32).reshape(1, 1, hidden), (1, 8, hidden))
    pl.semaphore_wait(barrier, len(partners))

    def span(start, size):
        return pl.ds(pl.multiple_of(start, 16), size)

    mine, by_x, by_y, diag = 2 * yy + xx, 2 * yy + (1 - xx), 2 * (1 - yy) + xx, 2 * (1 - yy) + (1 - xx)

    def rows_of(w, h, q):
        size = w.shape[0] // (GROUP * PARTS)
        return span(((core * PARTS + h) * 4 + q) * size, size)

    def wblock(i, s, h, q):
        return weights[i].at[s, rows_of(weights[i].at[0], h, q)]

    def wpart(i, s, h, c):
        size = weights[i].shape[1] // (2 * PARTS)
        return weights[i].at[s, span((c * PARTS + h) * size, size)]

    def goes_up(f):
        return m < n - 1 if f == 0 else (shard[f] < m) & (m < n - 1)

    def goes_down(f):
        return m > 0 if f == 0 else (shard[f] > m) & (m > 0)

    def along(f, src, dst, rsem):
        send(src, dst(slot_up[f]), zs.at[0, f], rsem(slot_up[f]), up, goes_up(f))
        send(src, dst(slot_down[f]), zs.at[1, f], rsem(slot_down[f]), down, goes_down(f))

    def along_block(f, src, i, h):
        along(f, src, lambda t: wblock(i, t, h, mine), lambda t: zr.at[i, h, t])

    def along_diag(f, src, i, h):
        along(f, src, lambda t: wblock(i, t, h, diag), lambda t: dr.at[h, t])

    def init():
        for i, w in enumerate((win_hbm, wout_hbm)):
            for h in range(PARTS):
                along_block(0, w.at[rows_of(w, h, mine)], i, h)
            if i == 0:
                for t, dev in enumerate(others):
                    t_slot = pick(m, [held[(mm + t + 1) % n].index(mm) for mm in range(n)])
                    send(bias.at[0], bias.at[t_slot], s_b, once.at[0], dev)

    def dg(i, h):
        w = (win_hbm, wout_hbm)[i]
        along_diag(0, w.at[rows_of(w, h, diag)], i, h)

    def df(k, i, h):
        f = k + 1
        block = wblock(i, f, h, diag)

        @pl.when(goes_up(f) | goes_down(f))
        def _():
            arrived(block, dr.at[h, f])

        along_diag(f, block, i, h)

    def e1(k, i, h):
        f = k + 1
        block = wblock(i, f, h, mine)
        arrived(block, zr.at[i, h, f])
        send(block, block, s_xy, (xr, xyr)[i].at[k, h], to_x)
        send(block, block, s_xy, (yr, xyr)[i].at[k, h], to_y)
        along_block(f, block, i, h)

    def e2(k, i, h):
        if i == 1:
            return
        f = k + 1
        if h % 2 == 0:
            block = wblock(i, f, h, by_x)
            arrived(block, xr.at[k, h])
            send(block, block, s_f, fr.at[k, h], to_y)
        else:
            block = wblock(i, f, h, by_y)
            arrived(block, yr.at[k, h])
            send(block, block, s_f, fr.at[k, h], to_x)

    def e3(k, i, h):
        f = k + 1
        if i == 0:
            if h % 2 == 0:
                arrived(wblock(i, f, h, by_y), yr.at[k, h])
            else:
                arrived(wblock(i, f, h, by_x), xr.at[k, h])
            arrived(wblock(i, f, h, diag), fr.at[k, h])
        else:
            arrived(wout.at[f, pl.ds(0, 2 * piece)], xyr.at[k, h])

            @pl.when(jnp.logical_not(goes_up(f) | goes_down(f)))
            def _():
                arrived(wblock(i, f, h, diag), dr.at[h, f])

        block = wpart(i, f, h, core)
        send(block, block, s_c, cr.at[k, i], to_core)

    def e4(k, i):
        arrived(weights[i].at[k + 1, span((1 - core) * half, half)], cr.at[k, i])
        if i == 0 and k == 0:
            arrived(bias.at[pl.ds(0, n - 1)], once.at[0])

    def mix_feat(b):
        if b == 0:
            loads[0].wait()
            loads[1].wait()
        r = slice(b * BLOCK, (b + 1) * BLOCK)
        for c in tiles:
            by[0:BLOCK, c] = mm(tok[r, :], feat[:, c]).astype(BF16)
            c2 = slice(c.start + width, c.stop + width)
            by[BLOCK : 2 * BLOCK, c] = mm(tok[r, :], feat[:, c2]).astype(BF16)

    def mix_seq(b):
        if b == 0:
            loads[2].wait()
        r = slice(b * BLOCK, (b + 1) * BLOCK)
        k = kind[b]
        for c in tiles:
            xhat[r, c] = tok[r, c].astype(F32) + mm(seq[k], by[:, c])

    def mix_norm(b):
        def norm_one(i, _):
            q = pl.ds(pl.multiple_of(b * BLOCK + i * RT, RT), RT)
            v = xhat[q, :]
            centre = v - jnp.mean(v, axis=-1, keepdims=True)
            rs = lax.rsqrt(jnp.mean(centre * centre, axis=-1, keepdims=True) + 1e-5)
            h = centre * rs
            xhat[q, :] = h
            rstd[q, :] = rs
            low = (h * g1 + s1).astype(BF16)
            xg[q, :] = low
            xt[:, q] = low.T
            return 0

        lax.fori_loop(0, BLOCK // RT, norm_one, 0)
        if b == blocks - 1:
            loads[5].start()

    def fwd_a(f, t):
        if f == 0 and t == 0:
            loads[3].wait()
        c = htiles[t]
        pre = mm(xg[...], win[f, :, c]) + bias[f, 0:1, c]
        a, dv = gelu_both(pre)
        hid[f, :, c] = a.astype(BF16)
        slope[f, :, c] = dv.astype(BF16)

    def fwd_b(f, t):
        if f == 0 and t == 0:
            loads[4].wait()
        c = tiles[t]
        term = mm(hid[f], wout[f, :, c])
        acc[:, c] = term if f == 0 else acc[:, c] + term

    zero = jnp.zeros((8, width), F32)
    def norm_two():
        loads[5].wait()

        def step(i, sums):
            q = pl.ds(pl.multiple_of(i * RT, RT), RT)
            v = xhat[q, :] * g1 + s1 + (acc[q, :] + bo)
            centre = v - jnp.mean(v, axis=-1, keepdims=True)
            rs = lax.rsqrt(jnp.mean(centre * centre, axis=-1, keepdims=True) + 1e-5)
            h = centre * rs
            tok[q, :] = (h * g2 + s2).astype(BF16)
            cot = by[q, :].astype(F32)
            dh = cot * g2
            gr = rs * (dh - jnp.mean(dh, axis=-1, keepdims=True) - h * jnp.mean(dh * h, axis=-1, keepdims=True))
            acc[q, :] = gr
            low = gr.astype(BF16)
            xg[q, :] = low
            gt[:, q] = low.T
            return (sums[0] + fold(low.astype(F32)), sums[1] + fold(cot * h), sums[2] + fold(cot))

        sums = lax.fori_loop(0, rows // RT, step, (zero, zero, zero))
        va[0] = jnp.zeros((16, width), F32)
        for i, v in enumerate(sums):
            va[0, 2 + i : 3 + i, :] = jnp.sum(v, axis=0, keepdims=True)

    near, far_half = span(core * half, half), span((1 - core) * half, half)

    def unit(j):
        k, i = j // 2, j % 2
        return pout.at[k] if i == 0 else hid.at[slot[k]]

    def part_rows(h, b, size):
        return span(core * half + h * (half // PARTS) + b * piece, size)

    def give(p, j):
        for h in range(PARTS):
            size = half // PARTS
            src = p.at[span((1 - core) * half + h * size, size)]
            send(src, r0.at[j, pl.ds(h * size, size)], s_h, hr.at[j, h], to_core)

    def unit_out(k, q):
        f = slot[k]
        for c in htiles:
            pout[k, q, c] = mm(gt[q, :], hid[f, :, c]).astype(BF16)

    def out_far(k):
        unit_out(k, far_half)
        give(pout.at[k], 2 * k)

    def out_near(k):
        unit_out(k, near)

    def unit_pre(k, t):
        f = slot[k]
        c = htiles[t]
        gp = (mm_t(xg[...], wout[f, c, :]) * slope[f, :, c].astype(F32)).astype(BF16)
        slope[f, :, c] = gp
        va[0, pl.ds(5 + target[k], 1), c] = jnp.sum(fold(gp.astype(F32)), axis=0, keepdims=True)

    def unit_in(k, q):
        f = slot[k]
        for c in htiles:
            hid[f, q, c] = mm(xt[q, :], slope[f, :, c]).astype(BF16)

    def in_far(k):
        unit_in(k, far_half)
        give(hid.at[slot[k]], 2 * k + 1)

    def in_near(k):
        unit_in(k, near)

    def add(a, b):
        return (a.astype(F32) + b.astype(F32)).astype(BF16)

    def u1(k, i, h):
        j = 2 * k + i
        p = unit(j)
        size = half // PARTS
        arrived(r0.at[j, pl.ds(h * size, size)], hr.at[j, h])
        for b, at, dev in ((1 - xx, 0, to_x), (2 + (1 - yy), 1, to_y)):
            q = part_rows(h, b, piece)
            p[q, :] = add(p[q, :], r0[j, span(h * size + b * piece, piece), :])
            send(p.at[q], rxy.at[j, h, at], s_t, tr.at[j, h], dev)

    def z_send(j, h, cond):
        k, i = j // 2, j % 2
        s = target[k]
        below = lax.div(n - 1 + m - s, n)
        last = 1 - lax.div(lax.rem(m - s - 1 + n, n) + (n - 1), n)
        slot = s + (n - s) * last
        send(rxy.at[j, h], rz.at[i, h, s], s_u, ur.at[i, h, s], up, cond & (below == 0))
        send(rxy.at[j, h], rz.at[i, h, slot], s_u, ur.at[i, h, slot], down, cond & (below == 1))

    def at_end(s):
        return ((s > m) & (m == 0)) | ((s < m) & (m == n - 1))

    def u2(k, i, h):
        j = 2 * k + i
        p = unit(j)
        size = half // PARTS
        arrived(rxy.at[j, h], tr.at[j, h])
        for b, at in ((xx, 0), (2 + yy, 1)):
            here = p[part_rows(h, b, piece), :].astype(F32) + r0[j, span(h * size + b * piece, piece), :].astype(F32)
            rxy[j, h, at] = (here + rxy[j, h, at].astype(F32)).astype(BF16)
        if k < n - 1:
            z_send(j, h, at_end(target[k]))

    def z_take(j, h, slot, cond):
        i = j % 2

        @pl.when(cond)
        def _():
            arrived(rz.at[i, h, slot], ur.at[i, h, slot])
            rxy[j, h] = add(rxy[j, h], rz[i, h, slot])

    def u3(k, i, h):
        j = 2 * k + i
        s = target[k]
        if k < n - 1:
            inner = jnp.logical_not(at_end(s))
            z_take(j, h, s, inner)
            z_send(j, h, inner)
        else:
            z_take(j, h, m, m > 0)
            z_take(j, h, n, m < n - 1)
            send(rxy.at[j, h, 0], rf.at[i, h, 0], s_fa, far.at[i, h], to_y)
            send(rxy.at[j, h, 1], rf.at[i, h, 1], s_fa, far.at[i, h], to_x)

    def fblock(i, h, b):
        return finals[i].at[part_rows(h, b, piece)]

    def f2(k, i, h):
        j = 2 * k + i
        arrived(rf.at[i, h], far.at[i, h])
        for b, at, dev in ((xx, 0, to_x), (2 + yy, 1, to_y)):
            block = fblock(i, h, b)
            block[...] = add(rxy[j, h, at], rf[i, h, at])
            send(block, block, s_fa, fbr.at[i, h], dev)

    def f3(k, i, h):
        arrived(rf.at[i, h], fbr.at[i, h])
        block = finals[i].at[part_rows(h, 0, half // PARTS)]
        send(block, block, s_fc, fcr.at[i], to_core)

    def f4(k, i):
        arrived(finals[i].at[far_half], fcr.at[i])
        if i == 0:
            for a in tiles:
                for c in htiles:
                    dwout[c, a] = fin[a, c].T

    def back_x(t):
        c = tiles[t]
        total = acc[:, c]
        for s in range(n):
            total = total + mm_t(slope[s], win[s, c, :])
        acc[:, c] = total

    def norm_one_back(t):
        def step(i, sums):
            q = pl.ds(pl.multiple_of(i * RT, RT), RT)
            gn = acc[q, :]
            h = xhat[q, :]
            dh = gn * g1
            gs = rstd[q, :] * (dh - jnp.mean(dh, axis=-1, keepdims=True) - h * jnp.mean(dh * h, axis=-1, keepdims=True))
            acc[q, :] = gs
            xg[q, :] = gs.astype(BF16)
            return (sums[0] + fold(gn * h), sums[1] + fold(gn))

        steps = rows // RT
        start = (zero, zero) if t == 0 else (part[0:8, :], part[8:16, :])
        sums = lax.fori_loop(t * steps // 2, (t + 1) * steps // 2, step, start)
        for i, v in enumerate(sums):
            if t == 0:
                part[8 * i : 8 * i + 8, :] = v
            else:
                va[0, i : i + 1, :] = jnp.sum(v, axis=0, keepdims=True)

    def unmix_seq(b):
        r = slice(b * BLOCK, (b + 1) * BLOCK)
        k = kind[b]
        for c in tiles:
            by[0:BLOCK, c] = mm(seq[k, :, 0:BLOCK], xg[r, c]).astype(BF16)
            by[BLOCK : 2 * BLOCK, c] = mm(seq[k, :, BLOCK:], xg[r, c]).astype(BF16)

    def unmix_feat(b):
        r = slice(b * BLOCK, (b + 1) * BLOCK)
        for c in tiles:
            c2 = slice(c.start + width, c.stop + width)
            acc[r, c] = acc[r, c] + mm(by[0:BLOCK, :], feat[:, c]) + mm(by[BLOCK : 2 * BLOCK, :], feat[:, c2])

    def vec(t):
        if t > 0 and t < 4:
            arrived(vr.at[t - 1], vrr.at[t - 1])
            va[t] = va[t - 1] + vr[t - 1]
        if t < 3:
            send(va.at[t], vr.at[t], s_v, vrr.at[t], (to_core, to_x, to_y)[t])
        elif t == 3:
            vz[pl.ds(m, 1)] = va[pl.ds(3, 1)]
            for dev in others:
                send(va.at[3], vz.at[m], s_vz, once.at[1], dev)
        else:
            arrived(vz.at[pl.ds(0, n - 1)], once.at[1])
            total = vz[0]
            for s in range(1, n):
                total = total + vz[s]
            vec_out[...] = total
            vec_out[5:6, :] = vec_out[pl.ds(5 + m, 1), :]

    init()
    mix_feat(0)
    mix_seq(0)
    e1(0, 0, 0)
    mix_norm(0)
    e1(0, 0, 1)
    e1(1, 0, 0)
    mix_feat(1)
    e1(1, 0, 1)
    dg(1, 0)
    e2(0, 0, 0)
    e1(0, 1, 0)
    e2(0, 1, 0)
    dg(1, 1)
    e2(0, 0, 1)
    mix_seq(1)
    mix_norm(1)
    fwd_a(0, 0)
    e2(1, 0, 0)
    e2(1, 0, 1)
    e1(0, 1, 1)
    e1(2, 0, 0)
    fwd_a(0, 1)
    fwd_a(0, 2)
    fwd_b(0, 0)
    fwd_b(0, 1)
    fwd_b(0, 2)
    e1(2, 0, 1)
    e3(0, 0, 1)
    e3(0, 0, 0)
    df(0, 1, 0)
    e3(0, 1, 0)
    e1(1, 1, 1)
    e3(1, 0, 1)
    e3(1, 0, 0)
    df(0, 1, 1)
    e4(0, 0)
    e1(1, 1, 0)
    e2(1, 1, 1)
    df(1, 1, 0)
    e2(0, 1, 1)
    e3(0, 1, 1)
    fwd_a(1, 0)
    fwd_a(1, 1)
    fwd_a(1, 2)
    e2(2, 0, 0)
    e2(1, 1, 0)
    e4(1, 0)
    e4(0, 1)
    e2(2, 0, 1)
    e1(2, 1, 0)
    e2(2, 1, 0)
    df(1, 1, 1)
    fwd_b(1, 0)
    fwd_b(1, 1)
    fwd_b(1, 2)
    fwd_a(2, 0)
    fwd_a(2, 1)
    fwd_a(2, 2)
    e3(1, 1, 0)
    e3(1, 1, 1)
    e1(2, 1, 1)
    e3(2, 0, 1)
    df(2, 1, 0)
    e2(2, 1, 1)
    e3(2, 0, 0)
    df(2, 1, 1)
    e4(1, 1)
    fwd_b(2, 0)
    fwd_b(2, 1)
    fwd_b(2, 2)
    e3(2, 1, 0)
    e4(2, 0)
    e3(2, 1, 1)
    fwd_a(3, 0)
    fwd_a(3, 1)
    e4(2, 1)
    fwd_a(3, 2)
    fwd_b(3, 0)
    fwd_b(3, 1)
    fwd_b(3, 2)
    norm_two()
    out_far(0)
    out_far(1)
    out_near(0)
    u1(0, 0, 1)
    out_far(2)
    u1(0, 0, 0)
    unit_pre(3, 0)
    out_near(1)
    unit_pre(0, 0)
    u2(0, 0, 1)
    u1(1, 0, 0)
    out_far(3)
    u1(1, 0, 1)
    out_near(2)
    u2(0, 0, 0)
    unit_pre(0, 1)
    u1(2, 0, 0)
    out_near(3)
    unit_pre(0, 2)
    u1(3, 0, 1)
    u3(0, 0, 1)
    u2(1, 0, 0)
    in_far(0)
    u1(2, 0, 1)
    u2(2, 0, 0)
    in_near(0)
    u1(0, 1, 0)
    u3(0, 0, 0)
    unit_pre(1, 0)
    unit_pre(1, 1)
    u1(0, 1, 1)
    u1(3, 0, 0)
    unit_pre(1, 2)
    in_far(1)
    u3(2, 0, 0)
    u2(1, 0, 1)
    u3(1, 0, 1)
    in_near(1)
    unit_pre(2, 0)
    u3(1, 0, 0)
    u1(1, 1, 1)
    unit_pre(2, 1)
    unit_pre(2, 2)
    u1(1, 1, 0)
    in_far(2)
    u2(0, 1, 0)
    in_near(2)
    u2(2, 0, 1)
    u1(2, 1, 0)
    u3(2, 0, 1)
    unit_pre(3, 1)
    unit_pre(3, 2)
    u1(2, 1, 1)
    in_far(3)
    u2(0, 1, 1)
    in_near(3)
    u2(1, 1, 0)
    u1(3, 1, 0)
    u3(0, 1, 0)
    u2(1, 1, 1)
    u1(3, 1, 1)
    back_x(0)
    u2(3, 0, 0)
    u3(3, 0, 0)
    back_x(1)
    u3(0, 1, 1)
    u3(1, 1, 0)
    u2(3, 0, 1)
    u3(3, 0, 1)
    back_x(2)
    u2(2, 1, 0)
    u3(2, 1, 0)
    f2(3, 0, 0)
    norm_one_back(0)
    norm_one_back(1)
    vec(0)
    u3(1, 1, 1)
    u2(2, 1, 1)
    u3(2, 1, 1)
    vec(1)
    f2(3, 0, 1)
    f3(3, 0, 0)
    u2(3, 1, 1)
    unmix_seq(0)
    u2(3, 1, 0)
    vec(2)
    u3(3, 1, 0)
    unmix_feat(0)
    u3(3, 1, 1)
    vec(3)
    f3(3, 0, 1)
    f2(3, 1, 0)
    unmix_seq(1)
    f2(3, 1, 1)
    unmix_feat(1)
    f3(3, 1, 0)
    f4(3, 0)
    f3(3, 1, 1)
    vec(4)
    f4(3, 1)
    line = hid.at[0, pl.ds(0, 3 * PARTS * piece)]
    for f in range(n):
        pl.when(goes_up(f))(functools.partial(all_sent, line, zs.at[0, f]))
        pl.when(goes_down(f))(functools.partial(all_sent, line, zs.at[1, f]))
    for ref, sem in (
        (r0.at[pl.ds(0, n - 1)], s_xy), (hid.at[0, pl.ds(0, (n - 1) * PARTS * piece)], s_f), (win.at[pl.ds(0, n - 1)], s_c),
        (win, s_h), (r0.at[pl.ds(0, n)], s_t), (r0.at[pl.ds(0, n - 1)], s_u), (r0.at[pl.ds(0, 2)], s_fa),
        (r0.at[pl.ds(0, 2)], s_fc), (bias.at[pl.ds(0, n - 1)], s_b), (va.at[pl.ds(0, 3)], s_v), (vz.at[pl.ds(0, n - 1)], s_vz),
    ):
        all_sent(ref, sem)


def layer(n, kind, vectors, tokens, grad_out, feat, seq, w_in, w_out):
    rows, width = tokens.shape
    hidden = w_in.shape[1]
    half, piece, units = width // 2, width // (GROUP * PARTS), 2 * n
    any_spec = pl.BlockSpec(memory_space=pl.ANY)
    vmem = pl.BlockSpec(memory_space=pltpu.VMEM)
    dma = pltpu.SemaphoreType.DMA
    low = lambda *shape: pltpu.VMEM(shape, BF16)
    full = lambda *shape: pltpu.VMEM(shape, F32)
    return pl.pallas_call(
        functools.partial(layer_kernel, n),
        out_shape=(
            low(rows, width),
            full(rows, width),
            low(width, hidden),
            low(hidden, width),
            full(16, width),
        ),
        in_specs=[pl.BlockSpec(memory_space=pltpu.SMEM)] + [vmem] * 6 + [any_spec] * 6,
        out_specs=[vmem] * 5,
        scratch_shapes=[
            low(*feat.shape), low(*seq.shape), low(n, width, hidden), low(n, hidden, width),
            low(n, rows, hidden), low(n, rows, hidden), full(rows, width), low(rows, width),
            low(width, rows), low(width, rows), low(rows, width), full(rows, 1), full(n, 8, hidden), full(16, width),
            low(n, width, hidden), low(units, half, hidden), low(units, PARTS, 2, piece, hidden),
            low(2, PARTS, n + 1, 2, piece, hidden),
            low(2, PARTS, 2, piece, hidden), low(width, hidden), full(4, 16, width), full(3, 16, width), full(n, 16, width),
            dma((6,)), dma((11,)), dma((2, n)), dma((2, PARTS, n)), dma((PARTS, n)), dma((n - 1, PARTS)), dma((n - 1, PARTS)),
            dma((n - 1, PARTS)), dma((n - 1, PARTS)), dma((n - 1, 2)), dma((units, PARTS)), dma((units, PARTS)),
            dma((2, PARTS, n + 1)), dma((2, PARTS)), dma((2, PARTS)), dma((2,)), dma((3,)), dma((2,)),
        ],
        compiler_params=pltpu.CompilerParams(
            vmem_limit_bytes=VMEM_LIMIT, collective_id=0, has_side_effects=True
        ),
    )(kind, *vectors, tokens, grad_out, feat, seq, w_in, w_out)


def close_kernel(vec, out_in, gt_in, dwin_in, dwout_in, out, gt, dwin, dwout, *rest):
    vectors, (a, b, sems) = rest[:6], rest[6:]
    puts = [pltpu.make_async_copy(x, y, sems.at[i]) for i, (x, y) in enumerate(((gt_in, gt), (out_in, out), (a, dwin), (b, dwout)))]
    puts[0].start()
    puts[1].start()
    for p, x, y in ((puts[2], dwin_in, a), (puts[3], dwout_in, b)):
        y[...] = x[...].astype(F32)
        p.start()
    for i, v in enumerate(vectors):
        v[...] = vec[i, :]
    for p in puts:
        p.wait()


def close(vec, *arrays):
    vec, out, gt, dwin, dwout = (pltpu.with_memory_space_constraint(v, pltpu.VMEM) for v in (vec, *arrays))
    any_spec = pl.BlockSpec(memory_space=pl.ANY)
    vmem = pl.BlockSpec(memory_space=pltpu.VMEM)
    like = jax.ShapeDtypeStruct
    return pl.pallas_call(
        close_kernel,
        out_shape=[like(out.shape, BF16), like(gt.shape, F32), like(dwin.shape, F32), like(dwout.shape, F32)]
        + [like(vec.shape[1:], F32)] * 6,
        in_specs=[vmem] * 5,
        out_specs=[any_spec] * 4 + [vmem] * 6,
        scratch_shapes=[
            pltpu.VMEM(dwin.shape, F32), pltpu.VMEM(dwout.shape, F32), pltpu.SemaphoreType.DMA((4,)),
        ],
        compiler_params=pltpu.CompilerParams(vmem_limit_bytes=40 * 2**20),
    )(vec, out, gt, dwin, dwout)


def local(
    tokens, block_kind, ln1_gain, ln1_bias, w_in, b_in, w_out, b_out, ln2_gain, ln2_bias, grad_out
):
    n_dp, n_mp = lax.axis_size("dp"), lax.axis_size("mp")
    feat = jnp.asarray(feature_table(tokens.shape[1]))
    seq = jnp.asarray(sequence_table())
    out, gt, dwin, dwout, vec = layer(
        n_mp, block_kind, (ln1_gain, ln1_bias, b_out, ln2_gain, ln2_bias, b_in), tokens, grad_out, feat, seq, w_in, w_out
    )
    shift = GROUP
    while shift < n_dp:
        turn = [(i, i // (2 * shift) * (2 * shift) + (i + shift) % (2 * shift)) for i in range(n_dp)]
        dwin, dwout = dwin.astype(F32), dwout.astype(F32)
        dwin, dwout, vec = (v + lax.ppermute(v, "dp", turn) for v in (dwin, dwout, vec))
        shift *= 2
    out, gt, dwin, dwout, gain1, bias1, bias_out, gain2, bias2, bias_in = close(vec, out, gt, dwin, dwout)
    return (out, gt, gain1, bias1, dwin, bias_in, dwout, bias_out, gain2, bias2)


def solution(mesh):
    in_specs = (
        P(("dp", "mp"), None),
        P(("dp", "mp")),
        P(),
        P(),
        P(None, "mp"),
        P("mp"),
        P("mp", None),
        P(),
        P(),
        P(),
        P(("dp", "mp"), None),
    )
    out_specs = (
        P(("dp", "mp"), None),
        P(("dp", "mp"), None),
        P(),
        P(),
        P(None, "mp"),
        P("mp"),
        P("mp", None),
        P(),
        P(),
        P(),
    )
    return jax.shard_map(local, mesh=mesh, in_specs=in_specs, out_specs=out_specs, check_vma=False)
```

```python
import functools
import math

import jax
import jax.numpy as jnp
import numpy as np
from jax import lax
from jax.experimental import pallas as pl
from jax.experimental.pallas import tpu as pltpu
from jax.sharding import PartitionSpec as P

BLOCK = 512
NT = 256
RT = 256
VMEM_LIMIT = 57 * 2**20
F32 = jnp.float32
BF16 = jnp.bfloat16
SQRT_2_PI = math.sqrt(2.0 / math.pi)


def sequence_table():
    ids = np.arange(BLOCK)
    out = []
    for variant in range(3):
        n = BLOCK // 2**variant
        place, owner = ids % n, ids // n
        same = owner[:, None] == owner[None, :]
        angle = (place[:, None] * place[None, :] % n) * (2.0 * math.pi / n)
        factor = 1.0 / math.sqrt(n)
        cos = np.where(same, np.cos(angle) * factor, 0.0)
        sin = np.where(same, np.sin(angle) * factor, 0.0)
        out.append(np.concatenate([cos, -sin], axis=1))
    return np.stack(out).astype(np.float32).astype(BF16)


def feature_table(n):
    ids = np.arange(n)
    angle = (ids[:, None] * ids[None, :] % n) * (2.0 * math.pi / n)
    factor = 1.0 / math.sqrt(n)
    return np.concatenate([np.cos(angle), np.sin(angle)], axis=1).astype(np.float32).__mul__(np.float32(factor)).astype(BF16)


def mm(a, b):
    return lax.dot_general(a, b, (((1,), (0,)), ((), ())), preferred_element_type=F32)


def mm_t(a, b):
    return lax.dot_general(a, b, (((1,), (1,)), ((), ())), preferred_element_type=F32)


def fold(v):
    return jnp.sum(v.reshape(v.shape[0] // 8, 8, v.shape[1]), axis=0)


def gelu_both(v):
    sq = v * v
    t = jnp.tanh(SQRT_2_PI * v * (1.0 + 0.044715 * sq))
    u = 0.5 * (1.0 + t)
    slope = u + (0.5 * SQRT_2_PI) * v * (1.0 - t * t) * (1.0 + (3 * 0.044715) * sq)
    return v * u, slope

MESH = pl.DeviceIdType.MESH
GROUP = 8

PARTS = 2

def pick(i, table):
    n = len(table)
    total = jnp.int32(0)
    for k, v in enumerate(table):
        total = total + v * (1 - lax.div(lax.rem(i - k + n, n) + (n - 1), n))
    return total


def layer_kernel(
    n, kind, g1_ref, s1_ref, bo_ref, g2_ref, s2_ref, bin_ref, tok_hbm, go_hbm, feat_hbm, seq_hbm, win_hbm, wout_hbm,
    tok, acc, dwin, dwout, vec_out,
    feat, seq, win, wout, hid, slope, xhat, xg, xt, gt, by, rstd, bias, part,
    pout, r0, rxy, rz, rf, fin, va, vr, vz,
    load_sem, sent, zs, zr, dr, xr, yr, xyr, fr, cr, hr, tr, ur, far, fbr, fcr, vrr, once,
):
    rows, width = tok.shape
    hidden = win.shape[2]
    blocks = rows // BLOCK
    weights, finals = (win, wout), (fin, dwin)
    d, m = lax.axis_index("dp"), lax.axis_index("mp")
    core, xx, yy = lax.rem(d, 2), lax.rem(lax.div(d, 2), 2), lax.rem(lax.div(d, 4), 2)
    to_core, to_x, to_y = (d + 1 - 2 * core, m), (d + 2 - 4 * xx, m), (d + 4 - 8 * yy, m)
    others = [(d, lax.rem(m + t, n)) for t in range(1, n)]
    up, down = (d, m + 1), (d, m - 1)
    held = [[mm] + sorted((s for s in range(n) if s != mm), key=lambda s: (abs(s - mm), s)) for mm in range(n)]
    shard = [pick(m, [held[mm][f] for mm in range(n)]) for f in range(n)]

    ends_first = [sorted(range(n), key=lambda s: (-abs(s - mm), -abs(2 * s - n + 1))) for mm in range(n)]
    slot = [pick(m, [held[mm].index(ends_first[mm][k]) for mm in range(n)]) for k in range(n)]
    target = [pick(m, [ends_first[mm][k] for mm in range(n)]) for k in range(n)]

    def slot_at(step, f):
        return pick(m, [held[mm + step].index(held[mm][f]) if 0 <= mm + step < n else 0 for mm in range(n)])

    slot_up, slot_down = ([slot_at(step, f) for f in range(n)] for step in (1, -1))
    tiles = [slice(i * NT, (i + 1) * NT) for i in range(width // NT)]
    htiles = [slice(i * NT, (i + 1) * NT) for i in range(hidden // NT)]
    half = width // 2
    piece = half // (4 * PARTS)
    s_xy, s_f, s_c, s_h, s_t, s_u, s_fa, s_fc, s_b, s_v, s_vz = (sent.at[i] for i in range(11))

    def remote(src, dst, ssem, rsem, dev):
        return pltpu.make_async_remote_copy(
            src_ref=src, dst_ref=dst, send_sem=ssem, recv_sem=rsem, device_id=dev, device_id_type=MESH
        )

    def send(src, dst, ssem, rsem, dev, cond=None):
        copy = remote(src, dst, ssem, rsem, dev)
        if cond is None:
            copy.start()
        else:
            pl.when(cond)(copy.start)

    def all_sent(ref, sem):
        remote(ref, ref, sem, sem, to_core).wait_send()

    def arrived(dst, rsem):
        remote(dst, dst, rsem, rsem, to_core).wait_recv()

    barrier = pltpu.get_barrier_semaphore()
    partners = [to_core, to_x, to_y] + others
    for dev in partners:
        pl.semaphore_signal(barrier, inc=1, device_id=dev, device_id_type=MESH)
    loads = [
        pltpu.make_async_copy(a, b, load_sem.at[i])
        for i, (a, b) in enumerate(
            [(tok_hbm, tok), (feat_hbm, feat), (seq_hbm, seq), (win_hbm, win.at[0]), (wout_hbm, wout.at[0]), (go_hbm, by)]
        )
    ]
    for c in loads[:5]:
        c.start()
    g1, s1, bo, g2, s2 = (
        r[...].astype(F32).reshape(1, width) for r in (g1_ref, s1_ref, bo_ref, g2_ref, s2_ref)
    )
    bias[0:1] = jnp.broadcast_to(bin_ref[...].astype(F32).reshape(1, 1, hidden), (1, 8, hidden))
    pl.semaphore_wait(barrier, len(partners))

    def span(start, size):
        return pl.ds(pl.multiple_of(start, 16), size)

    mine, by_x, by_y, diag = 2 * yy + xx, 2 * yy + (1 - xx), 2 * (1 - yy) + xx, 2 * (1 - yy) + (1 - xx)

    def rows_of(w, h, q):
        size = w.shape[0] // (GROUP * PARTS)
        return span(((core * PARTS + h) * 4 + q) * size, size)

    def wblock(i, s, h, q):
        return weights[i].at[s, rows_of(weights[i].at[0], h, q)]

    def wpart(i, s, h, c):
        size = weights[i].shape[1] // (2 * PARTS)
        return weights[i].at[s, span((c * PARTS + h) * size, size)]

    def goes_up(f):
        return m < n - 1 if f == 0 else (shard[f] < m) & (m < n - 1)

    def goes_down(f):
        return m > 0 if f == 0 else (shard[f] > m) & (m > 0)

    def along(f, src, dst, rsem):
        send(src, dst(slot_up[f]), zs.at[0, f], rsem(slot_up[f]), up, goes_up(f))
        send(src, dst(slot_down[f]), zs.at[1, f], rsem(slot_down[f]), down, goes_down(f))

    def along_block(f, src, i, h):
        along(f, src, lambda t: wblock(i, t, h, mine), lambda t: zr.at[i, h, t])

    def along_diag(f, src, i, h):
        along(f, src, lambda t: wblock(i, t, h, diag), lambda t: dr.at[h, t])

    def init():
        for i, w in enumerate((win_hbm, wout_hbm)):
            for h in range(PARTS):
                along_block(0, w.at[rows_of(w, h, mine)], i, h)
            if i == 0:
                for t, dev in enumerate(others):
                    t_slot = pick(m, [held[(mm + t + 1) % n].index(mm) for mm in range(n)])
                    send(bias.at[0], bias.at[t_slot], s_b, once.at[0], dev)

    def dg(i, h):
        w = (win_hbm, wout_hbm)[i]
        along_diag(0, w.at[rows_of(w, h, diag)], i, h)

    def df(k, i, h):
        f = k + 1
        block = wblock(i, f, h, diag)

        @pl.when(goes_up(f) | goes_down(f))
        def _():
            arrived(block, dr.at[h, f])

        along_diag(f, block, i, h)

    def e1(k, i, h):
        f = k + 1
        block = wblock(i, f, h, mine)
        arrived(block, zr.at[i, h, f])
        send(block, block, s_xy, (xr, xyr)[i].at[k, h], to_x)
        send(block, block, s_xy, (yr, xyr)[i].at[k, h], to_y)
        along_block(f, block, i, h)

    def e2(k, i, h):
        if i == 1:
            return
        f = k + 1
        if h % 2 == 0:
            block = wblock(i, f, h, by_x)
            arrived(block, xr.at[k, h])
            send(block, block, s_f, fr.at[k, h], to_y)
        else:
            block = wblock(i, f, h, by_y)
            arrived(block, yr.at[k, h])
            send(block, block, s_f, fr.at[k, h], to_x)

    def e3(k, i, h):
        f = k + 1
        if i == 0:
            if h % 2 == 0:
                arrived(wblock(i, f, h, by_y), yr.at[k, h])
            else:
                arrived(wblock(i, f, h, by_x), xr.at[k, h])
            arrived(wblock(i, f, h, diag), fr.at[k, h])
        else:
            arrived(wout.at[f, pl.ds(0, 2 * piece)], xyr.at[k, h])

            @pl.when(jnp.logical_not(goes_up(f) | goes_down(f)))
            def _():
                arrived(wblock(i, f, h, diag), dr.at[h, f])

        block = wpart(i, f, h, core)
        send(block, block, s_c, cr.at[k, i], to_core)

    def e4(k, i):
        arrived(weights[i].at[k + 1, span((1 - core) * half, half)], cr.at[k, i])
        if i == 0 and k == 0:
            arrived(bias.at[pl.ds(0, n - 1)], once.at[0])

    def mix_feat(b):
        if b == 0:
            loads[0].wait()
            loads[1].wait()
        r = slice(b * BLOCK, (b + 1) * BLOCK)
        for c in tiles:
            by[0:BLOCK, c] = mm(tok[r, :], feat[:, c]).astype(BF16)
            c2 = slice(c.start + width, c.stop + width)
            by[BLOCK : 2 * BLOCK, c] = mm(tok[r, :], feat[:, c2]).astype(BF16)

    def mix_seq(b):
        if b == 0:
            loads[2].wait()
        r = slice(b * BLOCK, (b + 1) * BLOCK)
        k = kind[b]
        for c in tiles:
            xhat[r, c] = tok[r, c].astype(F32) + mm(seq[k], by[:, c])

    def mix_norm(b):
        def norm_one(i, _):
            q = pl.ds(pl.multiple_of(b * BLOCK + i * RT, RT), RT)
            v = xhat[q, :]
            centre = v - jnp.mean(v, axis=-1, keepdims=True)
            rs = lax.rsqrt(jnp.mean(centre * centre, axis=-1, keepdims=True) + 1e-5)
            h = centre * rs
            xhat[q, :] = h
            rstd[q, :] = rs
            low = (h * g1 + s1).astype(BF16)
            xg[q, :] = low
            xt[:, q] = low.T
            return 0

        lax.fori_loop(0, BLOCK // RT, norm_one, 0)
        if b == blocks - 1:
            loads[5].start()

    def fwd_a(f, t):
        if f == 0 and t == 0:
            loads[3].wait()
        c = htiles[t]
        pre = mm(xg[...], win[f, :, c]) + bias[f, 0:1, c]
        a, dv = gelu_both(pre)
        hid[f, :, c] = a.astype(BF16)
        slope[f, :, c] = dv.astype(BF16)

    def fwd_b(f, t):
        if f == 0 and t == 0:
            loads[4].wait()
        c = tiles[t]
        term = mm(hid[f], wout[f, :, c])
        acc[:, c] = term if f == 0 else acc[:, c] + term

    zero = jnp.zeros((8, width), F32)
    def norm_two():
        loads[5].wait()

        def step(i, sums):
            q = pl.ds(pl.multiple_of(i * RT, RT), RT)
            v = xhat[q, :] * g1 + s1 + (acc[q, :] + bo)
            centre = v - jnp.mean(v, axis=-1, keepdims=True)
            rs = lax.rsqrt(jnp.mean(centre * centre, axis=-1, keepdims=True) + 1e-5)
            h = centre * rs
            tok[q, :] = (h * g2 + s2).astype(BF16)
            cot = by[q, :].astype(F32)
            dh = cot * g2
            gr = rs * (dh - jnp.mean(dh, axis=-1, keepdims=True) - h * jnp.mean(dh * h, axis=-1, keepdims=True))
            acc[q, :] = gr
            low = gr.astype(BF16)
            xg[q, :] = low
            gt[:, q] = low.T
            return (sums[0] + fold(low.astype(F32)), sums[1] + fold(cot * h), sums[2] + fold(cot))

        sums = lax.fori_loop(0, rows // RT, step, (zero, zero, zero))
        va[0] = jnp.zeros((16, width), F32)
        for i, v in enumerate(sums):
            va[0, 2 + i : 3 + i, :] = jnp.sum(v, axis=0, keepdims=True)

    near, far_half = span(core * half, half), span((1 - core) * half, half)

    def unit(j):
        k, i = j // 2, j % 2
        return pout.at[k] if i == 0 else hid.at[slot[k]]

    def part_rows(h, b, size):
        return span(core * half + h * (half // PARTS) + b * piece, size)

    def give(p, j):
        for h in range(PARTS):
            size = half // PARTS
            src = p.at[span((1 - core) * half + h * size, size)]
            send(src, r0.at[j, pl.ds(h * size, size)], s_h, hr.at[j, h], to_core)

    def unit_out(k, q):
        f = slot[k]
        for c in htiles:
            pout[k, q, c] = mm(gt[q, :], hid[f, :, c]).astype(BF16)

    def out_far(k):
        unit_out(k, far_half)
        give(pout.at[k], 2 * k)

    def out_near(k):
        unit_out(k, near)

    def unit_pre(k, t):
        f = slot[k]
        c = htiles[t]
        gp = (mm_t(xg[...], wout[f, c, :]) * slope[f, :, c].astype(F32)).astype(BF16)
        slope[f, :, c] = gp
        va[0, pl.ds(5 + target[k], 1), c] = jnp.sum(fold(gp.astype(F32)), axis=0, keepdims=True)

    def unit_in(k, q):
        f = slot[k]
        for c in htiles:
            hid[f, q, c] = mm(xt[q, :], slope[f, :, c]).astype(BF16)

    def in_far(k):
        unit_in(k, far_half)
        give(hid.at[slot[k]], 2 * k + 1)

    def in_near(k):
        unit_in(k, near)

    def add(a, b):
        return (a.astype(F32) + b.astype(F32)).astype(BF16)

    def u1(k, i, h):
        j = 2 * k + i
        p = unit(j)
        size = half // PARTS
        arrived(r0.at[j, pl.ds(h * size, size)], hr.at[j, h])
        for b, at, dev in ((1 - xx, 0, to_x), (2 + (1 - yy), 1, to_y)):
            q = part_rows(h, b, piece)
            p[q, :] = add(p[q, :], r0[j, span(h * size + b * piece, piece), :])
            send(p.at[q], rxy.at[j, h, at], s_t, tr.at[j, h], dev)

    def z_send(j, h, cond):
        k, i = j // 2, j % 2
        s = target[k]
        below = lax.div(n - 1 + m - s, n)
        last = 1 - lax.div(lax.rem(m - s - 1 + n, n) + (n - 1), n)
        slot = s + (n - s) * last
        send(rxy.at[j, h], rz.at[i, h, s], s_u, ur.at[i, h, s], up, cond & (below == 0))
        send(rxy.at[j, h], rz.at[i, h, slot], s_u, ur.at[i, h, slot], down, cond & (below == 1))

    def at_end(s):
        return ((s > m) & (m == 0)) | ((s < m) & (m == n - 1))

    def u2(k, i, h):
        j = 2 * k + i
        p = unit(j)
        size = half // PARTS
        arrived(rxy.at[j, h], tr.at[j, h])
        for b, at in ((xx, 0), (2 + yy, 1)):
            here = p[part_rows(h, b, piece), :].astype(F32) + r0[j, span(h * size + b * piece, piece), :].astype(F32)
            rxy[j, h, at] = (here + rxy[j, h, at].astype(F32)).astype(BF16)
        if k < n - 1:
            z_send(j, h, at_end(target[k]))

    def z_take(j, h, slot, cond):
        i = j % 2

        @pl.when(cond)
        def _():
            arrived(rz.at[i, h, slot], ur.at[i, h, slot])
            rxy[j, h] = add(rxy[j, h], rz[i, h, slot])

    def u3(k, i, h):
        j = 2 * k + i
        s = target[k]
        if k < n - 1:
            inner = jnp.logical_not(at_end(s))
            z_take(j, h, s, inner)
            z_send(j, h, inner)
        else:
            z_take(j, h, m, m > 0)
            z_take(j, h, n, m < n - 1)
            send(rxy.at[j, h, 0], rf.at[i, h, 0], s_fa, far.at[i, h], to_y)
            send(rxy.at[j, h, 1], rf.at[i, h, 1], s_fa, far.at[i, h], to_x)

    def fblock(i, h, b):
        return finals[i].at[part_rows(h, b, piece)]

    def f2(k, i, h):
        j = 2 * k + i
        arrived(rf.at[i, h], far.at[i, h])
        for b, at, dev in ((xx, 0, to_x), (2 + yy, 1, to_y)):
            block = fblock(i, h, b)
            block[...] = add(rxy[j, h, at], rf[i, h, at])
            send(block, block, s_fa, fbr.at[i, h], dev)

    def f3(k, i, h):
        arrived(rf.at[i, h], fbr.at[i, h])
        block = finals[i].at[part_rows(h, 0, half // PARTS)]
        send(block, block, s_fc, fcr.at[i], to_core)

    def f4(k, i):
        arrived(finals[i].at[far_half], fcr.at[i])
        if i == 0:
            for a in tiles:
                for c in htiles:
                    dwout[c, a] = fin[a, c].T

    def back_x(t):
        c = tiles[t]
        total = acc[:, c]
        for s in range(n):
            total = total + mm_t(slope[s], win[s, c, :])
        acc[:, c] = total

    def norm_one_back(t):
        def step(i, sums):
            q = pl.ds(pl.multiple_of(i * RT, RT), RT)
            gn = acc[q, :]
            h = xhat[q, :]
            dh = gn * g1
            gs = rstd[q, :] * (dh - jnp.mean(dh, axis=-1, keepdims=True) - h * jnp.mean(dh * h, axis=-1, keepdims=True))
            acc[q, :] = gs
            xg[q, :] = gs.astype(BF16)
            return (sums[0] + fold(gn * h), sums[1] + fold(gn))

        steps = rows // RT
        start = (zero, zero) if t == 0 else (part[0:8, :], part[8:16, :])
        sums = lax.fori_loop(t * steps // 2, (t + 1) * steps // 2, step, start)
        for i, v in enumerate(sums):
            if t == 0:
                part[8 * i : 8 * i + 8, :] = v
            else:
                va[0, i : i + 1, :] = jnp.sum(v, axis=0, keepdims=True)

    def unmix_seq(b):
        r = slice(b * BLOCK, (b + 1) * BLOCK)
        k = kind[b]
        for c in tiles:
            by[0:BLOCK, c] = mm(seq[k, :, 0:BLOCK], xg[r, c]).astype(BF16)
            by[BLOCK : 2 * BLOCK, c] = mm(seq[k, :, BLOCK:], xg[r, c]).astype(BF16)

    def unmix_feat(b):
        r = slice(b * BLOCK, (b + 1) * BLOCK)
        for c in tiles:
            c2 = slice(c.start + width, c.stop + width)
            acc[r, c] = acc[r, c] + mm(by[0:BLOCK, :], feat[:, c]) + mm(by[BLOCK : 2 * BLOCK, :], feat[:, c2])

    def vec(t):
        if t > 0 and t < 4:
            arrived(vr.at[t - 1], vrr.at[t - 1])
            va[t] = va[t - 1] + vr[t - 1]
        if t < 3:
            send(va.at[t], vr.at[t], s_v, vrr.at[t], (to_core, to_x, to_y)[t])
        elif t == 3:
            vz[pl.ds(m, 1)] = va[pl.ds(3, 1)]
            for dev in others:
                send(va.at[3], vz.at[m], s_vz, once.at[1], dev)
        else:
            arrived(vz.at[pl.ds(0, n - 1)], once.at[1])
            total = vz[0]
            for s in range(1, n):
                total = total + vz[s]
            vec_out[...] = total
            vec_out[5:6, :] = vec_out[pl.ds(5 + m, 1), :]

    init()
    mix_feat(0)
    mix_seq(0)
    e1(0, 0, 0)
    mix_norm(0)
    e1(0, 0, 1)
    e1(1, 0, 0)
    mix_feat(1)
    e1(1, 0, 1)
    dg(1, 0)
    e2(0, 0, 0)
    e1(0, 1, 0)
    e2(0, 1, 0)
    dg(1, 1)
    e2(0, 0, 1)
    mix_seq(1)
    mix_norm(1)
    fwd_a(0, 0)
    e2(1, 0, 0)
    e2(1, 0, 1)
    e1(0, 1, 1)
    e1(2, 0, 0)
    fwd_a(0, 1)
    fwd_a(0, 2)
    fwd_b(0, 0)
    fwd_b(0, 1)
    fwd_b(0, 2)
    e1(2, 0, 1)
    e3(0, 0, 1)
    e3(0, 0, 0)
    df(0, 1, 0)
    e3(0, 1, 0)
    e1(1, 1, 1)
    e3(1, 0, 1)
    e3(1, 0, 0)
    df(0, 1, 1)
    e4(0, 0)
    e1(1, 1, 0)
    e2(1, 1, 1)
    df(1, 1, 0)
    e2(0, 1, 1)
    e3(0, 1, 1)
    fwd_a(1, 0)
    fwd_a(1, 1)
    fwd_a(1, 2)
    e2(2, 0, 0)
    e2(1, 1, 0)
    e4(1, 0)
    e4(0, 1)
    e2(2, 0, 1)
    e1(2, 1, 0)
    e2(2, 1, 0)
    df(1, 1, 1)
    fwd_b(1, 0)
    fwd_b(1, 1)
    fwd_b(1, 2)
    fwd_a(2, 0)
    fwd_a(2, 1)
    fwd_a(2, 2)
    e3(1, 1, 0)
    e3(1, 1, 1)
    e1(2, 1, 1)
    e3(2, 0, 1)
    df(2, 1, 0)
    e2(2, 1, 1)
    e3(2, 0, 0)
    df(2, 1, 1)
    e4(1, 1)
    fwd_b(2, 0)
    fwd_b(2, 1)
    fwd_b(2, 2)
    e3(2, 1, 0)
    e4(2, 0)
    e3(2, 1, 1)
    fwd_a(3, 0)
    fwd_a(3, 1)
    e4(2, 1)
    fwd_a(3, 2)
    fwd_b(3, 0)
    fwd_b(3, 1)
    fwd_b(3, 2)
    norm_two()
    out_far(0)
    out_near(0)
    unit_pre(0, 0)
    u1(0, 0, 0)
    out_far(1)
    u1(0, 0, 1)
    out_near(1)
    out_far(2)
    unit_pre(0, 1)
    u2(0, 0, 0)
    u1(1, 0, 1)
    unit_pre(0, 2)
    in_far(0)
    u1(1, 0, 0)
    u2(0, 0, 1)
    in_near(0)
    u1(0, 1, 0)
    out_far(3)
    u1(0, 1, 1)
    out_near(2)
    unit_pre(2, 0)
    u3(0, 0, 0)
    u2(1, 0, 0)
    unit_pre(1, 0)
    u1(2, 0, 0)
    unit_pre(2, 1)
    u1(2, 0, 1)
    u2(1, 0, 1)
    unit_pre(2, 2)
    unit_pre(1, 1)
    out_near(3)
    u1(3, 0, 1)
    in_far(2)
    unit_pre(1, 2)
    u3(1, 0, 0)
    u3(0, 0, 1)
    u1(3, 0, 0)
    in_far(1)
    in_near(2)
    u2(0, 1, 1)
    u1(2, 1, 0)
    unit_pre(3, 0)
    unit_pre(3, 1)
    u2(2, 0, 1)
    u3(2, 0, 1)
    u1(2, 1, 1)
    in_near(1)
    u3(1, 0, 1)
    u1(1, 1, 0)
    unit_pre(3, 2)
    in_far(3)
    u1(1, 1, 1)
    u2(0, 1, 0)
    u2(2, 0, 0)
    u3(0, 1, 1)
    in_near(3)
    u1(3, 1, 0)
    u1(3, 1, 1)
    u2(3, 0, 0)
    u2(3, 0, 1)
    u3(2, 0, 0)
    back_x(0)
    u3(3, 0, 1)
    u2(1, 1, 1)
    u3(1, 1, 1)
    u3(0, 1, 0)
    back_x(1)
    u2(1, 1, 0)
    u3(3, 0, 0)
    u2(2, 1, 1)
    f2(3, 0, 1)
    back_x(2)
    u3(2, 1, 1)
    f2(3, 0, 0)
    u3(1, 1, 0)
    norm_one_back(0)
    norm_one_back(1)
    vec(0)
    u2(2, 1, 0)
    u3(2, 1, 0)
    f3(3, 0, 1)
    u2(3, 1, 1)
    vec(1)
    f3(3, 0, 0)
    unmix_seq(0)
    u3(3, 1, 1)
    vec(2)
    unmix_feat(0)
    u2(3, 1, 0)
    u3(3, 1, 0)
    f2(3, 1, 1)
    vec(3)
    unmix_seq(1)
    f2(3, 1, 0)
    unmix_feat(1)
    f4(3, 0)
    f3(3, 1, 1)
    f3(3, 1, 0)
    vec(4)
    f4(3, 1)
    line = hid.at[0, pl.ds(0, 3 * PARTS * piece)]
    for f in range(n):
        pl.when(goes_up(f))(functools.partial(all_sent, line, zs.at[0, f]))
        pl.when(goes_down(f))(functools.partial(all_sent, line, zs.at[1, f]))
    for ref, sem in (
        (r0.at[pl.ds(0, n - 1)], s_xy), (hid.at[0, pl.ds(0, (n - 1) * PARTS * piece)], s_f), (win.at[pl.ds(0, n - 1)], s_c),
        (win, s_h), (r0.at[pl.ds(0, n)], s_t), (r0.at[pl.ds(0, n - 1)], s_u), (r0.at[pl.ds(0, 2)], s_fa),
        (r0.at[pl.ds(0, 2)], s_fc), (bias.at[pl.ds(0, n - 1)], s_b), (va.at[pl.ds(0, 3)], s_v), (vz.at[pl.ds(0, n - 1)], s_vz),
    ):
        all_sent(ref, sem)


def layer(n, kind, vectors, tokens, grad_out, feat, seq, w_in, w_out):
    rows, width = tokens.shape
    hidden = w_in.shape[1]
    half, piece, units = width // 2, width // (GROUP * PARTS), 2 * n
    any_spec = pl.BlockSpec(memory_space=pl.ANY)
    vmem = pl.BlockSpec(memory_space=pltpu.VMEM)
    dma = pltpu.SemaphoreType.DMA
    low = lambda *shape: pltpu.VMEM(shape, BF16)
    full = lambda *shape: pltpu.VMEM(shape, F32)
    return pl.pallas_call(
        functools.partial(layer_kernel, n),
        out_shape=(
            low(rows, width),
            full(rows, width),
            low(width, hidden),
            low(hidden, width),
            full(16, width),
        ),
        in_specs=[pl.BlockSpec(memory_space=pltpu.SMEM)] + [vmem] * 6 + [any_spec] * 6,
        out_specs=[vmem] * 5,
        scratch_shapes=[
            low(*feat.shape), low(*seq.shape), low(n, width, hidden), low(n, hidden, width),
            low(n, rows, hidden), low(n, rows, hidden), full(rows, width), low(rows, width),
            low(width, rows), low(width, rows), low(rows, width), full(rows, 1), full(n, 8, hidden), full(16, width),
            low(n, width, hidden), low(units, half, hidden), low(units, PARTS, 2, piece, hidden),
            low(2, PARTS, n + 1, 2, piece, hidden),
            low(2, PARTS, 2, piece, hidden), low(width, hidden), full(4, 16, width), full(3, 16, width), full(n, 16, width),
            dma((6,)), dma((11,)), dma((2, n)), dma((2, PARTS, n)), dma((PARTS, n)), dma((n - 1, PARTS)), dma((n - 1, PARTS)),
            dma((n - 1, PARTS)), dma((n - 1, PARTS)), dma((n - 1, 2)), dma((units, PARTS)), dma((units, PARTS)),
            dma((2, PARTS, n + 1)), dma((2, PARTS)), dma((2, PARTS)), dma((2,)), dma((3,)), dma((2,)),
        ],
        compiler_params=pltpu.CompilerParams(
            vmem_limit_bytes=VMEM_LIMIT, collective_id=0, has_side_effects=True
        ),
    )(kind, *vectors, tokens, grad_out, feat, seq, w_in, w_out)


def close_kernel(vec, out_in, gt_in, dwin_in, dwout_in, out, gt, dwin, dwout, *rest):
    vectors, (a, b, sems) = rest[:6], rest[6:]
    puts = [pltpu.make_async_copy(x, y, sems.at[i]) for i, (x, y) in enumerate(((gt_in, gt), (out_in, out), (a, dwin), (b, dwout)))]
    puts[0].start()
    puts[1].start()
    for p, x, y in ((puts[2], dwin_in, a), (puts[3], dwout_in, b)):
        y[...] = x[...].astype(F32)
        p.start()
    for i, v in enumerate(vectors):
        v[...] = vec[i, :]
    for p in puts:
        p.wait()


def close(vec, *arrays):
    vec, out, gt, dwin, dwout = (pltpu.with_memory_space_constraint(v, pltpu.VMEM) for v in (vec, *arrays))
    any_spec = pl.BlockSpec(memory_space=pl.ANY)
    vmem = pl.BlockSpec(memory_space=pltpu.VMEM)
    like = jax.ShapeDtypeStruct
    return pl.pallas_call(
        close_kernel,
        out_shape=[like(out.shape, BF16), like(gt.shape, F32), like(dwin.shape, F32), like(dwout.shape, F32)]
        + [like(vec.shape[1:], F32)] * 6,
        in_specs=[vmem] * 5,
        out_specs=[any_spec] * 4 + [vmem] * 6,
        scratch_shapes=[
            pltpu.VMEM(dwin.shape, F32), pltpu.VMEM(dwout.shape, F32), pltpu.SemaphoreType.DMA((4,)),
        ],
        compiler_params=pltpu.CompilerParams(vmem_limit_bytes=40 * 2**20),
    )(vec, out, gt, dwin, dwout)


def local(
    tokens, block_kind, ln1_gain, ln1_bias, w_in, b_in, w_out, b_out, ln2_gain, ln2_bias, grad_out
):
    n_dp, n_mp = lax.axis_size("dp"), lax.axis_size("mp")
    feat = jnp.asarray(feature_table(tokens.shape[1]))
    seq = jnp.asarray(sequence_table())
    out, gt, dwin, dwout, vec = layer(
        n_mp, block_kind, (ln1_gain, ln1_bias, b_out, ln2_gain, ln2_bias, b_in), tokens, grad_out, feat, seq, w_in, w_out
    )
    shift = GROUP
    while shift < n_dp:
        turn = [(i, i // (2 * shift) * (2 * shift) + (i + shift) % (2 * shift)) for i in range(n_dp)]
        dwin, dwout = dwin.astype(F32), dwout.astype(F32)
        dwin, dwout, vec = (v + lax.ppermute(v, "dp", turn) for v in (dwin, dwout, vec))
        shift *= 2
    out, gt, dwin, dwout, gain1, bias1, bias_out, gain2, bias2, bias_in = close(vec, out, gt, dwin, dwout)
    return (out, gt, gain1, bias1, dwin, bias_in, dwout, bias_out, gain2, bias2)


def solution(mesh):
    in_specs = (
        P(("dp", "mp"), None),
        P(("dp", "mp")),
        P(),
        P(),
        P(None, "mp"),
        P("mp"),
        P("mp", None),
        P(),
        P(),
        P(),
        P(("dp", "mp"), None),
    )
    out_specs = (
        P(("dp", "mp"), None),
        P(("dp", "mp"), None),
        P(),
        P(),
        P(None, "mp"),
        P("mp"),
        P("mp", None),
        P(),
        P(),
        P(),
    )
    return jax.shard_map(local, mesh=mesh, in_specs=in_specs, out_specs=out_specs, check_vma=False)
```
